128 devices in a mesh: section: 16 (over x_hi, y, core), row: 8 (over z, x_lo).
Axes of the slice: x: 4 (x_hi: 2, x_lo: 2; x = x_hi * 2 + x_lo), y: 4, z: 4, core: 2. Of those that a mesh axis runs over, the one named last changes fastest.
Arguments:
- hidden: bfloat16 [16, 16, 4, 3072], P('section', 'row'), may hold values from -6 to 6
- cond: bfloat16 [3072], replicated, may hold values from -6 to 6
- mod_weight: bfloat16 [3072, 6144], P(None, ('section', 'row')), may hold values from -0.109375 to 0.109375
- mod_bias: bfloat16 [6144], P(('section', 'row')), may hold values from -1.1953125 to 1.1953125
- proj_weight: bfloat16 [3072, 64], replicated, may hold values from -0.109375 to 0.109375
- proj_bias: bfloat16 [64], replicated, may hold values from -1.1953125 to 1.1953125
- latent_cache: bfloat16 [2, 32, 8, 16], P(None, 'row'), may hold values from -6 to 6
- in_weight: bfloat16 [432, 512], replicated, may hold values from -0.3125 to 0.3125
- in_bias: bfloat16 [512], replicated, may hold values from -1.1953125 to 1.1953125
- conv_weight: bfloat16 [16, 13824, 512], P('section'), may hold values from -0.02734375 to 0.02734375
- conv_bias: bfloat16 [16, 512], P('section'), may hold values from -1.1953125 to 1.1953125
- conv_cache: bfloat16 [16, 2, 32, 8, 512], P('section', None, 'row'), may hold values from -3 to 3
- final_weight: bfloat16 [13824, 512], P(None, 'section'), may hold values from -0.0546875 to 0.0546875
- final_bias: bfloat16 [512], P('section'), may hold values from -1.1953125 to 1.1953125
- final_cache: bfloat16 [2, 32, 8, 512], P(None, 'row'), may hold values from -3 to 3
Outputs:
- decoded: bfloat16 [16, 32, 8, 512], P(None, 'row', None, 'section')
- new_cache: bfloat16 [16, 2, 32, 8, 512], P('section', None, 'row')
The draws below stay inside these ranges and needn't reach their ends.
All inputs are finite; a program needn't handle non-finite values.
Results may differ from the reference program's by a relative error of at most 0.035.
Values may be sent and summed in bfloat16 or wider, within the bound.
No kernel may reach another device: no remote copies, remote signals or barrier semaphores. Data moves between devices by JAX's collectives and lax.ppermute only.
A program may use at most 64 MiB of HBM per device.

```python
import jax
import jax.numpy as jnp
from jax import lax

D = 3072
C_LAT = 16
CH = 512
WL = 8
FRAMES = 16
LAYERS = 16
HL = 32
HT = 16
WT = 4


def steps_of(rng, shape, shards, smallest, high):
    factor_of, own = 1.0, jax.random.fold_in(rng, 6)
    for axis_at, blocks in shards:
        heights = jnp.exp(jax.random.uniform(jax.random.fold_in(own, axis_at), (blocks,), jnp.float32, smallest / len(shards), high / len(shards)))
        factor_of = factor_of * jnp.repeat(heights, shape[axis_at] // blocks).reshape([-1 if axis == axis_at else 1 for axis in range(len(shape))])
    return factor_of


def normal_values(stream_key, dims, spread, limit, cuts=(), held_as=jnp.bfloat16):
    entries = jax.random.normal(stream_key, dims, jnp.float32) * spread
    if len(cuts) > 0:
        entries = steps_of(stream_key, dims, cuts, -0.22, 0.18) * entries
    return jnp.clip(entries, min=-limit, max=limit).astype(held_as)


def setup_inputs(seed: int = 0) -> dict:
    arg_keys = jax.random.split(jax.random.key(seed), 16)
    hidden = normal_values(arg_keys[0], (FRAMES, HT, WT, D), 1.0, 6.0, ((0, 16), (1, 8)))
    cond = normal_values(arg_keys[1], (D,), 1.0, 6.0)
    mod_weight = normal_values(arg_keys[2], (D, 2 * D), D ** -0.5, 0.109375, ((1, 128),))
    mod_bias = normal_values(arg_keys[3], (2 * D,), 0.2, 1.1953125, ((0, 128),))
    proj_weight = normal_values(arg_keys[4], (D, 4 * C_LAT), D ** -0.5, 0.109375)
    proj_bias = normal_values(arg_keys[5], (4 * C_LAT,), 0.2, 1.1953125)
    latent_cache = normal_values(arg_keys[6], (2, HL, WL, C_LAT), 1.0, 6.0, ((1, 8),))
    in_weight = normal_values(arg_keys[7], (27 * C_LAT, CH), (27 * C_LAT) ** -0.5, 0.3125)
    in_bias = normal_values(arg_keys[8], (CH,), 0.2, 1.1953125)
    conv_weight = normal_values(arg_keys[9], (LAYERS, 27 * CH, CH), (4 * 27 * CH) ** -0.5, 0.02734375, ((0, 16),))
    conv_bias = normal_values(arg_keys[10], (LAYERS, CH), 0.2, 1.1953125, ((0, 16),))
    conv_cache = normal_values(arg_keys[11], (LAYERS, 2, HL, WL, CH), 0.5, 3.0, ((0, 16), (2, 8)))
    final_weight = normal_values(arg_keys[12], (27 * CH, CH), (27 * CH) ** -0.5, 0.0546875, ((1, 16),))
    final_bias = normal_values(arg_keys[13], (CH,), 0.2, 1.1953125, ((0, 16),))
    final_cache = normal_values(arg_keys[14], (2, HL, WL, CH), 0.5, 3.0, ((1, 8),))
    return dict(hidden=hidden, cond=cond, mod_weight=mod_weight, mod_bias=mod_bias, proj_weight=proj_weight, proj_bias=proj_bias, latent_cache=latent_cache, in_weight=in_weight, in_bias=in_bias, conv_weight=conv_weight, conv_bias=conv_bias, conv_cache=conv_cache, final_weight=final_weight, final_bias=final_bias, final_cache=final_cache)


def pad_grid(tensor):
    return jnp.pad(tensor, ((0, 0), (1, 1), (1, 1), (0, 0)))

def conv_stack(sequence, frame_count, weight):
    row_count = sequence.shape[1] - 2
    col_count = sequence.shape[2] - 2
    pieces = [sequence[time_off:time_off + frame_count, row_off:row_off + row_count, col_off:col_off + col_count, :] for time_off in range(3) for row_off in range(3) for col_off in range(3)]
    patches = jnp.concatenate(pieces, axis=-1).reshape(frame_count * row_count * col_count, -1)
    return jnp.dot(patches, weight, preferred_element_type=jnp.float32)

def causal_conv(cache_frames, frames, weight):
    sequence = pad_grid(jnp.concatenate([cache_frames, frames], axis=0))
    frame_count = frames.shape[0]
    outcome = conv_stack(sequence, frame_count, weight)
    return outcome.reshape(frame_count, frames.shape[1], frames.shape[2], -1)

def activate(tensor):
    return jax.nn.silu(tensor.astype(jnp.float32)).astype(jnp.bfloat16)

def reference(hidden, cond, mod_weight, mod_bias, proj_weight, proj_bias, latent_cache, in_weight, in_bias, conv_weight, conv_bias, conv_cache, final_weight, final_bias, final_cache):
    modulation = jnp.dot(activate(cond)[None], mod_weight, preferred_element_type=jnp.float32)[0] + mod_bias.astype(jnp.float32)
    shift_part = modulation[:D]
    scale_part = modulation[D:]
    values = hidden.astype(jnp.float32)
    average = lax.optimization_barrier(jnp.mean(values, axis=-1, keepdims=True))
    centered = values - average
    variance = lax.optimization_barrier(jnp.mean(centered * centered, axis=-1, keepdims=True))
    normed = centered / jnp.sqrt(variance + 1e-06)
    modded = (normed * (1.0 + scale_part) + shift_part).astype(jnp.bfloat16)
    flattened = modded.reshape(-1, D)
    patches = (jnp.dot(flattened, proj_weight, preferred_element_type=jnp.float32) + proj_bias.astype(jnp.float32)).astype(jnp.bfloat16)
    latent = patches.reshape(FRAMES, HT, WT, C_LAT, 2, 2).transpose(0, 1, 4, 2, 5, 3).reshape(FRAMES, HL, WL, C_LAT)
    residual = (causal_conv(latent_cache, latent, in_weight) + in_bias.astype(jnp.float32)).astype(jnp.bfloat16)
    caches = []
    for layer_idx in range(LAYERS):
        activated = activate(residual)
        caches.append(activated[FRAMES - 2:])
        summed = residual.astype(jnp.float32) + causal_conv(conv_cache[layer_idx], activated, conv_weight[layer_idx])
        residual = (summed + conv_bias[layer_idx].astype(jnp.float32)).astype(jnp.bfloat16)
    last_activ = activate(residual)
    decoded = (causal_conv(final_cache, last_activ, final_weight) + final_bias.astype(jnp.float32)).astype(jnp.bfloat16)
    return (decoded, jnp.stack(caches))
```

```python
import functools

import jax
import jax.numpy as jnp
from jax import lax
from jax.experimental import pallas as pl
from jax.experimental.pallas import tpu as pltpu
from jax.sharding import PartitionSpec as P

AXES = ("section", "row")
SECTIONS = 16
ROWS = 8
STRIPE = 4
RING = ROWS * STRIPE
COLS = 8
CH = 512
CHUNK = 4
CHUNKS = 4
LANES = CHUNK * COLS
WINDOW = 8
WIDE = 6
TAP = 3 * CH
VMEM_LIMIT = 16 << 20
C_LAT = 16
ROW_LANES = COLS * C_LAT
FRAMES = SECTIONS


def device_of(section, row):
    return section * ROWS + row % ROWS


def live_sections(step):
    return [s for s in range(SECTIONS) if 0 <= step - s < CHUNKS]


def straight_pairs(step):
    return [
        (device_of(s, r), device_of(s + 1, r))
        for s in live_sections(step)
        if s < SECTIONS - 1
        for r in range(ROWS)
    ]


def slanted_pairs(step):
    pairs = []
    for s in live_sections(step):
        if s % 2 == 1 and s < SECTIONS - 1:
            shift = 1 if ((s + 1) // 2) % 2 == 1 else -1
            pairs += [(device_of(s, r), device_of(s + 1, r + shift)) for r in range(ROWS)]
    return pairs


def window_base(section, row):
    first = section % 2 == 0
    even = (section // 2) % 2 == 0
    base = jnp.where(first, jnp.where(even, 0, -2), jnp.where(even, 1, -1))
    return STRIPE * row + base, base


def block_step(
    step,
    has_entry,
    flags,
    *refs,
):
    if has_entry:
        entry, main, slant, *refs = refs
    elif step > 0:
        main, slant, *refs = refs
    (history, weight, bias, wide, narrow, history_out, window, taps, saved, total) = refs
    section = flags[0]
    first = flags[1]
    even = flags[2]
    seam = flags[3]
    live = jnp.logical_and(section <= step, section > step - CHUNKS)

    @pl.when(jnp.logical_not(live))
    def _():
        history_out[...] = history[...]

    @pl.when(live)
    def _():
        if has_entry:

            @pl.when(section == 0)
            def _():
                window[...] = entry[...]

        if step > 0:

            @pl.when(jnp.logical_and(section > 0, jnp.logical_and(first == 1, even == 1)))
            def _():
                window[:STRIPE] = main[:STRIPE]
                window[STRIPE:] = slant[...]

            @pl.when(jnp.logical_and(first == 1, even == 0))
            def _():
                window[:STRIPE] = slant[...]
                window[STRIPE:] = main[:STRIPE]

            @pl.when(first == 0)
            def _():
                window[:WIDE] = main[...]

        column = lax.broadcasted_iota(jnp.int32, ((CHUNK + 2) * COLS, CH), 0) % COLS
        zero = jnp.zeros(((CHUNK + 2) * COLS, CH), jnp.float32)

        def prepare(y, carry):
            value = window[y].astype(jnp.float32)
            active = (value / (1.0 + jnp.exp(-value))).astype(jnp.bfloat16)
            frames = jnp.concatenate(
                [history[y].astype(jnp.float32), active.astype(jnp.float32)], axis=0
            )
            history_out[y] = active[LANES - 2 * COLS :]
            before = jnp.where(column == 0, zero, pltpu.roll(frames, 1, 0))
            after = jnp.where(column == COLS - 1, zero, pltpu.roll(frames, (CHUNK + 2) * COLS - 1, 0))
            for e, shifted in enumerate((before, frames, after)):
                for a in range(3):
                    taps[a * 3 + e, y] = shifted[a * COLS : a * COLS + LANES].astype(jnp.bfloat16)
            return carry

        lax.fori_loop(0, jnp.where(first == 1, WINDOW, WIDE), prepare, 0)

        at_seam = jnp.logical_and(seam > 0, seam < WINDOW)

        def convolve(rows):
            size = rows * LANES
            total[:size] = window[1 : 1 + rows].astype(jnp.float32).reshape(size, CH) + bias[...]

            def add(b):
                def one(a, carry):
                    left = jnp.concatenate(
                        [taps[a * 3 + e, b : b + rows].reshape(size, CH) for e in range(3)], axis=-1
                    )
                    at = pl.multiple_of((9 * a + 3 * b) * CH, TAP)
                    total[:size] += jnp.dot(
                        left, weight[pl.ds(at, TAP), :], preferred_element_type=jnp.float32
                    )
                    return carry

                lax.fori_loop(0, 3, one, 0)

            add(1)

            @pl.when(at_seam)
            def _():
                saved[...] = taps[:, seam - 1]
                taps[:, seam - 1] = jnp.zeros((9, LANES, CH), jnp.bfloat16)

            add(0)

            @pl.when(at_seam)
            def _():
                taps[:, seam - 1] = saved[...]
                taps[:, seam] = jnp.zeros((9, LANES, CH), jnp.bfloat16)

            add(2)
            return total[:size].astype(jnp.bfloat16).reshape(rows, LANES, CH)

        @pl.when(first == 1)
        def _():
            wide[...] = convolve(WIDE)

        @pl.when(first == 0)
        def _():
            result = convolve(STRIPE)
            wide[:STRIPE] = result
            narrow[...] = result


def run_step(step, flags, entry, main, slant, history, weight, bias):
    has_entry = entry is not None
    arrays = [history, weight, bias]
    if step > 0:
        arrays = [main, slant] + arrays
    if has_entry:
        arrays = [entry] + ([] if step > 0 else [jnp.zeros((8, 128), jnp.bfloat16)] * 2) + arrays
    vmem = pl.BlockSpec(memory_space=pltpu.VMEM)
    return pl.pallas_call(
        functools.partial(block_step, step, has_entry),
        in_specs=[pl.BlockSpec(memory_space=pltpu.SMEM)] + [vmem] * len(arrays),
        out_specs=(vmem,) * 3,
        out_shape=(
            jax.ShapeDtypeStruct((WIDE, LANES, CH), jnp.bfloat16),
            jax.ShapeDtypeStruct((STRIPE, LANES, CH), jnp.bfloat16),
            jax.ShapeDtypeStruct((WINDOW, 2 * COLS, CH), jnp.bfloat16),
        ),
        scratch_shapes=[
            pltpu.VMEM((WINDOW, LANES, CH), jnp.bfloat16),
            pltpu.VMEM((9, WINDOW, LANES, CH), jnp.bfloat16),
            pltpu.VMEM((9, LANES, CH), jnp.bfloat16),
            pltpu.VMEM((WIDE * LANES, CH), jnp.float32),
        ],
        compiler_params=pltpu.CompilerParams(vmem_limit_bytes=VMEM_LIMIT),
        name="block_step",
    )(flags, *arrays)


def spread_weight_body(weight, spread):
    spread[...] = jnp.zeros_like(spread)
    for x in range(COLS):
        first, last = max(x - 1, 0), min(x + 1, COLS - 1)
        for ab in range(9):
            start = (3 * ab + first - x + 1) * C_LAT
            count = (last - first + 1) * C_LAT
            spread[x, ab * ROW_LANES + first * C_LAT : ab * ROW_LANES + first * C_LAT + count] = (
                weight[start : start + count]
            )


def spread_weight(weight):
    return pl.pallas_call(
        spread_weight_body,
        in_specs=[pl.BlockSpec(memory_space=pltpu.VMEM)],
        out_specs=pl.BlockSpec(memory_space=pltpu.VMEM),
        out_shape=jax.ShapeDtypeStruct((COLS, 9 * ROW_LANES, CH), jnp.bfloat16),
        compiler_params=pltpu.CompilerParams(vmem_limit_bytes=VMEM_LIMIT),
        cost_estimate=pl.CostEstimate(flops=0, bytes_accessed=10 << 20, transcendentals=0),
        name="spread_weight",
    )(weight)


def make_entries_body(spots, blocks, weight, bias, entries, upper, lower, left, total):
    section = spots[0]
    row = spots[1]

    @pl.when(section == 0)
    def _():
        def stripe(frame, shift):
            at = lax.rem(row + shift + ROWS, ROWS)
            if frame < 2:
                tile = blocks[at].astype(jnp.float32)
                return tile[STRIPE + frame * STRIPE : STRIPE + (frame + 1) * STRIPE]
            return blocks[(frame - 2) * ROWS + at].astype(jnp.float32)[:STRIPE]

        for frame in range(FRAMES + 2):
            before = stripe(frame, -1)[STRIPE - 1 :]
            own = stripe(frame, 0)
            after = stripe(frame, 1)
            later = stripe(frame, 2)[:1]
            before = jnp.where(row == 0, jnp.zeros_like(before), before)
            below = jnp.where(row == ROWS - 1, jnp.zeros_like(before), after[:1])
            above = jnp.where(row == ROWS - 1, jnp.zeros_like(before), own[STRIPE - 1 :])
            later = jnp.where(row == ROWS - 2, jnp.zeros_like(before), later)
            rows = [before] + [own[i : i + 1] for i in range(STRIPE)] + [below]
            for i in range(STRIPE + 2):
                upper[i, frame : frame + 1] = rows[i]
            rows = [above] + [after[i : i + 1] for i in range(STRIPE)] + [later]
            for i in range(STRIPE + 2):
                lower[i, frame : frame + 1] = rows[i]
        for y in range(WINDOW):
            source = upper if y < STRIPE else lower
            for a in range(3):
                for b in range(3):
                    piece = source[y % STRIPE + b, a : a + FRAMES]
                    at = (3 * a + b) * ROW_LANES
                    left[y * FRAMES : (y + 1) * FRAMES, at : at + ROW_LANES] = piece.astype(
                        jnp.bfloat16
                    )

        def column(x, carry):
            value = jnp.dot(left[...], weight[x], preferred_element_type=jnp.float32) + bias[...]
            for q in range(CH // 128):
                total[q, pl.ds(x, WINDOW * FRAMES, stride=COLS), :] = value[:, q * 128 : q * 128 + 128]
            return carry

        for x in range(COLS):
            column(x, 0)
        for c in range(CHUNKS):
            for y in range(WINDOW):
                at = (y * FRAMES + c * CHUNK) * COLS
                for q in range(CH // 128):
                    entries[c, y, :, q * 128 : q * 128 + 128] = total[q, at : at + LANES].astype(
                        jnp.bfloat16
                    )


def make_entries(spots, blocks, weight, bias):
    vmem = pl.BlockSpec(memory_space=pltpu.VMEM)
    return pl.pallas_call(
        make_entries_body,
        in_specs=[pl.BlockSpec(memory_space=pltpu.SMEM)] + [vmem] * 3,
        out_specs=vmem,
        out_shape=jax.ShapeDtypeStruct((CHUNKS, WINDOW, LANES, CH), jnp.bfloat16),
        scratch_shapes=[
            pltpu.VMEM((STRIPE + 2, FRAMES + 8, ROW_LANES), jnp.float32),
            pltpu.VMEM((STRIPE + 2, FRAMES + 8, ROW_LANES), jnp.float32),
            pltpu.VMEM((WINDOW * FRAMES, 9 * ROW_LANES), jnp.bfloat16),
            pltpu.VMEM((CH // 128, WINDOW * FRAMES * COLS, 128), jnp.float32),
        ],
        compiler_params=pltpu.CompilerParams(vmem_limit_bytes=VMEM_LIMIT),
        name="make_entries",
    )(spots, blocks, weight, bias)


def neighbour_rows(value, shift):
    return lax.ppermute(
        value,
        AXES,
        [(device_of(s, r), device_of(s, r + shift)) for s in range(SECTIONS) for r in range(ROWS)],
    )


def spread(value):
    section_at = lax.axis_index("section")
    holders = [SECTIONS - 1]
    for bit in (8, 4, 2, 1):
        fresh = [s ^ bit for s in holders]
        pairs = [
            (device_of(s, r), device_of(s ^ bit, r)) for s in holders for r in range(ROWS)
        ]
        moved = lax.ppermute(value, AXES, pairs)
        is_fresh = functools.reduce(jnp.logical_or, [section_at == s for s in fresh])
        value = jnp.where(is_fresh, moved, value)
        holders += fresh
    return value


def conv_stack(sequence, frame_count, weight):
    row_count = sequence.shape[1] - 2
    col_count = sequence.shape[2] - 2
    pieces = [
        sequence[
            time_off : time_off + frame_count,
            row_off : row_off + row_count,
            col_off : col_off + col_count,
            :,
        ]
        for time_off in range(3)
        for row_off in range(3)
        for col_off in range(3)
    ]
    patches = jnp.concatenate(pieces, axis=-1).reshape(frame_count * row_count * col_count, -1)
    return jnp.dot(patches, weight, preferred_element_type=jnp.float32)


def activate(tensor):
    return jax.nn.silu(tensor.astype(jnp.float32)).astype(jnp.bfloat16)


def to_everyone(value):
    count = SECTIONS * ROWS
    copies = jnp.broadcast_to(value, (count,) + value.shape[1:])
    return lax.all_to_all(copies, AXES, 0, 0, tiled=True)


def local(
    hidden,
    cond,
    mod_weight,
    mod_bias,
    proj_weight,
    proj_bias,
    latent_cache,
    in_weight,
    in_bias,
    conv_weight,
    conv_bias,
    conv_cache,
    final_weight,
    final_bias,
    final_cache,
):
    section_at = lax.axis_index("section")
    row_at = lax.axis_index("row")
    model_width = hidden.shape[-1]
    own_terms = jnp.dot(activate(cond)[None], mod_weight, preferred_element_type=jnp.float32)[
        0
    ] + mod_bias.astype(jnp.float32)
    own_count = own_terms.shape[0]
    padded_terms = jnp.pad(own_terms, (0, 128 - own_count))[None, None]
    modulation = to_everyone(padded_terms)[:, 0, :own_count].reshape(-1)
    shift_part = modulation[:model_width]
    scale_part = modulation[model_width:]
    values = hidden.astype(jnp.float32)
    average = jnp.mean(values, axis=-1, keepdims=True)
    centered = values - average
    variance = jnp.mean(centered * centered, axis=-1, keepdims=True)
    normed = centered / jnp.sqrt(variance + 1e-06)
    modded = (normed * (1.0 + scale_part) + shift_part).astype(jnp.bfloat16)
    patches = (
        jnp.dot(modded.reshape(-1, model_width), proj_weight, preferred_element_type=jnp.float32)
        + proj_bias.astype(jnp.float32)
    ).astype(jnp.bfloat16)
    lat_chan = latent_cache.shape[-1]
    own_latent = patches.reshape(1, hidden.shape[1], hidden.shape[2], lat_chan, 2, 2)
    own_latent = own_latent.transpose(0, 1, 4, 2, 5, 3).reshape(1, STRIPE, COLS * lat_chan)
    latent_old = latent_cache.reshape(1, 2 * STRIPE, COLS * lat_chan)
    blocks = to_everyone(jnp.concatenate([own_latent, latent_old, own_latent], axis=1))
    spots = jnp.stack([section_at, row_at]).astype(jnp.int32)
    entries = make_entries(spots, blocks, spread_weight(in_weight), in_bias.astype(jnp.float32)[None])
    frame_count = SECTIONS
    at_end = row_at == ROWS - 1

    base, offset = window_base(section_at, row_at)
    flags = jnp.stack(
        [
            section_at,
            jnp.where(section_at % 2 == 0, 1, 0),
            jnp.where((section_at // 2) % 2 == 0, 1, 0),
            (2 * RING - base) % RING,
        ]
    ).astype(jnp.int32)
    own_cache = conv_cache[0].transpose(1, 0, 2, 3).reshape(STRIPE, 2 * COLS, CH)
    around_cache = jnp.concatenate(
        [
            neighbour_rows(own_cache, 1),
            own_cache,
            neighbour_rows(own_cache, -1),
            jnp.zeros((1, 2 * COLS, CH), jnp.bfloat16),
        ],
        axis=0,
    )
    history = lax.dynamic_slice_in_dim(around_cache, STRIPE + offset, WINDOW, axis=0)
    layer_weight = conv_weight[0]
    layer_bias = conv_bias.astype(jnp.float32)

    main = slant = None
    finished = []
    for step in range(SECTIONS + CHUNKS - 1):
        entry = entries[step] if step < CHUNKS else None
        wide, narrow, history = run_step(
            step, flags, entry, main, slant, history, layer_weight, layer_bias
        )
        if step >= SECTIONS - 1:
            finished.append(narrow)
        if step < SECTIONS + CHUNKS - 2:
            main = lax.ppermute(wide, AXES, straight_pairs(step))
            pairs = slanted_pairs(step)
            if pairs:
                slant = lax.ppermute(narrow, AXES, pairs)
            else:
                slant = jnp.zeros_like(narrow)

    above = lax.ppermute(
        history[3:4],
        AXES,
        [
            (device_of(s, r), device_of(s, r + 1))
            for s in range(SECTIONS)
            if s % 4 == 1
            for r in range(ROWS)
        ],
    )
    widened = jnp.concatenate([above, history], axis=0)
    new_cache = lax.dynamic_slice_in_dim(widened, 1 - offset, STRIPE, axis=0)
    new_cache = new_cache.reshape(STRIPE, 2, COLS, CH).transpose(1, 0, 2, 3)[None]

    arrived = spread(jnp.concatenate(finished, axis=1))
    arrived = arrived.reshape(STRIPE, frame_count, COLS, CH).transpose(1, 0, 2, 3)
    tail = jnp.concatenate([final_cache, activate(arrived)], axis=0)
    top = neighbour_rows(tail[:, -1:], 1)
    bottom = neighbour_rows(tail[:, :1], -1)
    top = jnp.where(row_at == 0, jnp.zeros_like(top), top)
    bottom = jnp.where(at_end, jnp.zeros_like(bottom), bottom)
    rimmed = jnp.concatenate([top, tail, bottom], axis=1)
    rimmed = jnp.pad(rimmed, ((0, 0), (0, 0), (1, 1), (0, 0)))
    decoded = conv_stack(rimmed, frame_count, final_weight) + final_bias.astype(jnp.float32)
    decoded = decoded.astype(jnp.bfloat16).reshape(frame_count, STRIPE, COLS, -1)
    return (decoded, new_cache)


def solution(mesh):
    placed = (
        P("section", "row", None, None),
        P(),
        P(None, ("section", "row")),
        P(("section", "row")),
        P(),
        P(),
        P(None, "row", None, None),
        P(),
        P(),
        P("section", None, None),
        P("section", None),
        P("section", None, "row", None, None),
        P(None, "section"),
        P("section"),
        P(None, "row", None, None),
    )
    return jax.shard_map(
        local,
        mesh=mesh,
        in_specs=placed,
        out_specs=(P(None, "row", None, "section"), P("section", None, "row", None, None)),
        check_vma=False,
    )
```

```python
import functools

import jax
import jax.numpy as jnp
from jax import lax
from jax.experimental import pallas as pl
from jax.experimental.pallas import tpu as pltpu
from jax.sharding import PartitionSpec as P

AXES = ("section", "row")
SECTIONS = 16
ROWS = 8
STRIPE = 4
RING = ROWS * STRIPE
COLS = 8
CH = 512
CHUNK = 4
CHUNKS = 4
LANES = CHUNK * COLS
WINDOW = 8
WIDE = 6
TAP = 3 * CH
VMEM_LIMIT = 24 << 20
ENTRY_VMEM = 14 << 20
STEP_VMEM = 8 << 20
STAGES = SECTIONS // 2
LAST = SECTIONS - 2
SPREAD_FROM = LAST
C_LAT = 16
ROW_LANES = COLS * C_LAT
FRAMES = SECTIONS


def device_of(section, row):
    return section * ROWS + row % ROWS


def sending_stages(step):
    group = step // 4 * 4
    steps = range(group, group + 4) if step < SPREAD_FROM else (step,)
    return [j for j in range(STAGES - 1) if any(0 <= t - 2 * j < CHUNKS for t in steps)]


def straight_pairs(step):
    return [
        (device_of(2 * j, r), device_of(2 * j + 2, r))
        for j in sending_stages(step)
        for r in range(ROWS)
    ]


def slanted_pairs(step):
    return [
        (device_of(2 * j, r), device_of(2 * j + 2, r + (1 if j % 2 == 0 else -1)))
        for j in sending_stages(step)
        for r in range(ROWS)
    ]


def prepare_rows(count, window, history, history_out, taps):
    lanes = window.shape[1]
    size = lanes + 2 * COLS
    column = lax.broadcasted_iota(jnp.int32, (size, CH), 0) % COLS
    zero = jnp.zeros((size, CH), jnp.float32)

    def prepare(y):
        value = window[y].astype(jnp.float32)
        active = (value / (1.0 + jnp.exp(-value))).astype(jnp.bfloat16)
        frames = jnp.concatenate(
            [history[y].astype(jnp.float32), active.astype(jnp.float32)], axis=0
        )
        history_out[y] = active[lanes - 2 * COLS :]
        before = jnp.where(column == 0, zero, pltpu.roll(frames, 1, 0))
        after = jnp.where(column == COLS - 1, zero, pltpu.roll(frames, size - 1, 0))
        for e, shifted in enumerate((before, frames, after)):
            for a in range(3):
                taps[a * 3 + e, y] = shifted[a * COLS : a * COLS + lanes].astype(jnp.bfloat16)

    def pair(i, carry):
        prepare(2 * i)
        prepare(2 * i + 1)
        return carry

    lax.fori_loop(0, count // 2, pair, 0)


def convolve(rows, seam, taps, saved, total, weight):
    size = rows * LANES

    def add(b):
        def one(a, carry):
            left = jnp.concatenate(
                [taps[a * 3 + e, b : b + rows].reshape(size, CH) for e in range(3)], axis=-1
            )
            at = pl.multiple_of((9 * a + 3 * b) * CH, TAP)
            total[:size] += jnp.dot(
                left, weight[pl.ds(at, TAP), :], preferred_element_type=jnp.float32
            )
            return carry

        lax.fori_loop(0, 3, one, 0)

    add(1)
    at_seam = jnp.logical_and(seam > 0, seam < rows + 2)

    @pl.when(at_seam)
    def _():
        saved[...] = taps[:, seam - 1]
        taps[:, seam - 1] = jnp.zeros((9, LANES, CH), jnp.bfloat16)

    add(0)

    @pl.when(at_seam)
    def _():
        taps[:, seam - 1] = saved[...]
        taps[:, seam] = jnp.zeros((9, LANES, CH), jnp.bfloat16)

    add(2)


def first_block(seam, window, history, new, bias, weight, scratch):
    middle, taps, saved, total = scratch
    prepare_rows(WINDOW, window, history, new, taps)
    inner = window[1 : 1 + WIDE].astype(jnp.float32).reshape(WIDE * LANES, CH)
    total[...] = inner + bias[...]
    convolve(WIDE, seam, taps, saved, total, weight)
    middle[...] = total[...].astype(jnp.bfloat16).reshape(WIDE, LANES, CH)


def second_block(seam, out, history, new, bias, weight, scratch):
    middle, taps, saved, total = scratch
    size = STRIPE * LANES
    prepare_rows(WIDE, middle, history, new, taps)
    inner = middle[1 : 1 + STRIPE].astype(jnp.float32).reshape(size, CH)
    total[:size] = inner + bias[...]
    convolve(STRIPE, seam - 1, taps, saved, total, weight)
    out[...] = total[:size].astype(jnp.bfloat16).reshape(STRIPE, LANES, CH)


STEP_SCRATCH = [
    pltpu.VMEM((WINDOW, LANES, CH), jnp.bfloat16),
    pltpu.VMEM((WIDE, LANES, CH), jnp.bfloat16),
    pltpu.VMEM((9, WINDOW, LANES, CH), jnp.bfloat16),
    pltpu.VMEM((9, LANES, CH), jnp.bfloat16),
    pltpu.VMEM((WIDE * LANES, CH), jnp.float32),
]


def pair_step(step, has_entry, has_hop, flags, *refs):
    refs = list(refs)
    entry = refs.pop(0) if has_entry else None
    main, slant = (refs.pop(0), refs.pop(0)) if has_hop else (None, None)
    (history_a, history_b, weight_a, weight_b, bias_a, bias_b) = refs[:6]
    (out, new_a, new_b, window, middle, taps, saved, total) = refs[6:]
    section = flags[0]
    leans_down = flags[1]
    seam = flags[2]
    chunk = step - section

    @pl.when(jnp.logical_and(section % 2 == 0, jnp.logical_and(chunk >= 0, chunk < CHUNKS)))
    def _():
        if has_entry:

            @pl.when(section == 0)
            def _():
                window[...] = entry[...]

        if has_hop:

            @pl.when(jnp.logical_and(section > 0, leans_down == 1))
            def _():
                window[:STRIPE] = main[...]
                window[STRIPE:] = slant[...]

            @pl.when(leans_down == 0)
            def _():
                window[:STRIPE] = slant[...]
                window[STRIPE:] = main[...]

        scratch = (middle, taps, saved, total)
        first_block(seam, window, history_a, new_a, bias_a, weight_a, scratch)
        second_block(seam, out, history_b, new_b, bias_b, weight_b, scratch)


def run_step(step, flags, entry, main, slant, history_a, history_b, *weights):
    has_entry = entry is not None
    has_hop = main is not None
    arrays = ([entry] if has_entry else []) + ([main, slant] if has_hop else [])
    at = 1 + len(arrays)
    arrays += [history_a, history_b, *weights]
    vmem = pl.BlockSpec(memory_space=pltpu.VMEM)
    flops = 2 * (WIDE + STRIPE) * LANES * 27 * CH * CH
    return pl.pallas_call(
        functools.partial(pair_step, step, has_entry, has_hop),
        in_specs=[pl.BlockSpec(memory_space=pltpu.SMEM)] + [vmem] * len(arrays),
        out_specs=(vmem,) * 3,
        out_shape=(
            jax.ShapeDtypeStruct((STRIPE, LANES, CH), jnp.bfloat16),
            jax.ShapeDtypeStruct(history_a.shape, jnp.bfloat16),
            jax.ShapeDtypeStruct(history_b.shape, jnp.bfloat16),
        ),
        input_output_aliases={at: 1, at + 1: 2},
        scratch_shapes=STEP_SCRATCH,
        compiler_params=pltpu.CompilerParams(vmem_limit_bytes=STEP_VMEM),
        cost_estimate=pl.CostEstimate(flops=flops, bytes_accessed=1 << 20, transcendentals=0),
        name="pair_step",
    )(flags, *arrays)


def make_entries(section, row, blocks, weight, bias, entries, rows, padded, left, total):
    @pl.when(section == 0)
    def _():
        def stripe(frame, shift):
            at = lax.rem(row + shift + ROWS, ROWS)
            if frame < 2:
                tile = blocks[at].astype(jnp.float32)
                return tile[STRIPE + frame * STRIPE : STRIPE + (frame + 1) * STRIPE]
            return blocks[(frame - 2) * ROWS + at].astype(jnp.float32)[:STRIPE]

        for frame in range(FRAMES + 2):
            before = stripe(frame, -1)[STRIPE - 1 :]
            own = stripe(frame, 0)
            next_one = stripe(frame, 1)
            later = stripe(frame, 2)[:1]
            zero = jnp.zeros_like(before)
            before = jnp.where(row == 0, zero, before)
            below = jnp.where(row == ROWS - 1, zero, next_one[:1])
            above = jnp.where(row == ROWS - 1, zero, own[STRIPE - 1 :])
            later = jnp.where(row == ROWS - 2, zero, later)
            pieces = [before] + [own[i : i + 1] for i in range(STRIPE)] + [below]
            pieces += [above] + [next_one[i : i + 1] for i in range(STRIPE)] + [later]
            for i, piece in enumerate(pieces):
                rows[i, frame : frame + 1] = piece
        padded[...] = jnp.zeros_like(padded)
        for ab in range(9):
            padded[ab * ROW_LANES : ab * ROW_LANES + 3 * C_LAT] = weight[
                ab * 3 * C_LAT : (ab + 1) * 3 * C_LAT
            ]
        lane = lax.broadcasted_iota(jnp.int32, (FRAMES, ROW_LANES), 1)
        count = WINDOW * FRAMES

        def arrange(y, carry):
            for ab in range(9):
                first = y + 2 * (y // STRIPE) + ab % 3
                piece = rows[first, ab // 3 : ab // 3 + FRAMES]
                for x in range(COLS):
                    moved = piece if x == 1 else pltpu.roll(piece, (1 - x) * C_LAT % ROW_LANES, 1)
                    if x == 0:
                        moved = jnp.where(lane < C_LAT, jnp.zeros_like(moved), moved)
                    if x == COLS - 1:
                        moved = jnp.where(lane >= 2 * C_LAT, jnp.zeros_like(moved), moved)
                    at = pl.multiple_of(x * count + y * FRAMES, FRAMES)
                    left[pl.ds(at, FRAMES), ab * ROW_LANES : (ab + 1) * ROW_LANES] = moved.astype(
                        jnp.bfloat16
                    )
            return carry

        lax.fori_loop(0, WINDOW, arrange, 0)
        for x in range(0, COLS, 2):
            value = jnp.dot(
                left[x * count : (x + 2) * count], padded[...], preferred_element_type=jnp.float32
            )
            value = value + bias[...]
            for half in range(2):
                part = value[half * count : (half + 1) * count]
                for q in range(CH // 128):
                    total[q, pl.ds(x + half, count, stride=COLS), :] = part[
                        :, q * 128 : q * 128 + 128
                    ]
        for c in range(CHUNKS):
            for y in range(WINDOW):
                at = (y * FRAMES + c * CHUNK) * COLS
                for q in range(CH // 128):
                    entries[c, y, :, q * 128 : q * 128 + 128] = total[q, at : at + LANES].astype(
                        jnp.bfloat16
                    )


def first_step_body(
    flags,
    blocks,
    in_weight,
    in_bias,
    far_a,
    far_b,
    history_a,
    history_b,
    bias_a,
    bias_b,
    out,
    new_a,
    new_b,
    entries,
    weight_a,
    weight_b,
    rows,
    padded,
    left,
    sums,
    window,
    middle,
    taps,
    saved,
    total,
    done,
):
    section = flags[0]
    seam = flags[2]
    scratch = (middle, taps, saved, total)
    copies = [
        pltpu.make_async_copy(far_a, weight_a, done.at[0]),
        pltpu.make_async_copy(far_b, weight_b, done.at[1]),
    ]
    for copy in copies:
        copy.start()
    make_entries(section, flags[3], blocks, in_weight, in_bias, entries, rows, padded, left, sums)
    copies[0].wait()

    @pl.when(section == 0)
    def _():
        window[...] = entries[0]
        first_block(seam, window, history_a, new_a, bias_a, weight_a, scratch)

    copies[1].wait()

    @pl.when(section == 0)
    def _():
        second_block(seam, out, history_b, new_b, bias_b, weight_b, scratch)


def first_step(flags, blocks, in_weight, in_bias, far_a, far_b, history_a, history_b, *biases):
    vmem = pl.BlockSpec(memory_space=pltpu.VMEM)
    hbm = pl.BlockSpec(memory_space=pltpu.HBM)
    return pl.pallas_call(
        first_step_body,
        in_specs=[pl.BlockSpec(memory_space=pltpu.SMEM)] + [vmem] * 3 + [hbm] * 2 + [vmem] * 4,
        out_specs=(vmem,) * 6,
        out_shape=(
            jax.ShapeDtypeStruct((STRIPE, LANES, CH), jnp.bfloat16),
            jax.ShapeDtypeStruct(history_a.shape, jnp.bfloat16),
            jax.ShapeDtypeStruct(history_b.shape, jnp.bfloat16),
            jax.ShapeDtypeStruct((CHUNKS, WINDOW, LANES, CH), jnp.bfloat16),
            pltpu.VMEM(far_a.shape, far_a.dtype),
            pltpu.VMEM(far_b.shape, far_b.dtype),
        ),
        input_output_aliases={6: 1, 7: 2},
        scratch_shapes=[
            pltpu.VMEM((2 * (STRIPE + 2), FRAMES + 8, ROW_LANES), jnp.float32),
            pltpu.VMEM((9 * ROW_LANES, CH), jnp.bfloat16),
            pltpu.VMEM((COLS * WINDOW * FRAMES, 9 * ROW_LANES), jnp.bfloat16),
            pltpu.VMEM((CH // 128, WINDOW * FRAMES * COLS, 128), jnp.float32),
            *STEP_SCRATCH,
            pltpu.SemaphoreType.DMA((2,)),
        ],
        compiler_params=pltpu.CompilerParams(vmem_limit_bytes=ENTRY_VMEM),
        name="first_step",
    )(
        flags,
        blocks,
        in_weight,
        in_bias,
        pltpu.with_memory_space_constraint(far_a, pltpu.HBM),
        pltpu.with_memory_space_constraint(far_b, pltpu.HBM),
        history_a,
        history_b,
        *biases,
    )


def final_body(frames, value, above, below, history, weight, bias, out, new, *scratch):
    (window, taps, total) = scratch
    lanes = frames * COLS
    size = STRIPE * lanes
    window[:1] = above[...]
    window[1 : 1 + STRIPE] = value[...]
    window[1 + STRIPE :] = below[...]
    prepare_rows(WIDE, window, history, new, taps)
    total[...] = jnp.broadcast_to(bias[...], total.shape)

    def one(ab, carry):
        a = ab // 3
        b = ab % 3
        left = jnp.concatenate(
            [taps[a * 3 + e, pl.ds(b, STRIPE)].reshape(size, CH) for e in range(3)], axis=-1
        )
        total[...] += lax.dot_general(
            left,
            weight[:, pl.ds(pl.multiple_of(ab * TAP, TAP), TAP)],
            (((1,), (1,)), ((), ())),
            preferred_element_type=jnp.float32,
        )
        return carry

    lax.fori_loop(0, 9, one, 0)
    for y in range(STRIPE):
        for f in range(frames):
            at = y * lanes + f * COLS
            out[f, y] = total[at : at + COLS].astype(jnp.bfloat16)


def final_part(frames, value, above, below, history, weight, bias):
    vmem = pl.BlockSpec(memory_space=pltpu.VMEM)
    lanes = frames * COLS
    channels = bias.shape[-1]
    return pl.pallas_call(
        functools.partial(final_body, frames),
        in_specs=[vmem] * 6,
        out_specs=(vmem, vmem),
        out_shape=(
            jax.ShapeDtypeStruct((frames, STRIPE, COLS, channels), jnp.bfloat16),
            jax.ShapeDtypeStruct(history.shape, jnp.bfloat16),
        ),
        scratch_shapes=[
            pltpu.VMEM((WIDE, lanes, CH), jnp.bfloat16),
            pltpu.VMEM((9, WIDE, lanes, CH), jnp.bfloat16),
            pltpu.VMEM((STRIPE * lanes, channels), jnp.float32),
        ],
        compiler_params=pltpu.CompilerParams(vmem_limit_bytes=VMEM_LIMIT),
        cost_estimate=pl.CostEstimate(
            flops=2 * STRIPE * lanes * 27 * CH * 256, bytes_accessed=1 << 20, transcendentals=0
        ),
        name="final_part",
    )(value, above, below, history, weight, bias)


EVENS = range(0, SECTIONS, 2)


def to_even(value):
    return lax.ppermute(
        value, AXES, [(device_of(s + 1, r), device_of(s, r)) for s in EVENS for r in range(ROWS)]
    )


def neighbour_rows(value, shift):
    return lax.ppermute(
        value,
        AXES,
        [(device_of(s, r), device_of(s, r + shift)) for s in range(SECTIONS) for r in range(ROWS)],
    )


def spread_plan():
    rounds = []
    for at in range(CHUNKS + 2):
        first, second = [], []
        if at < CHUNKS:
            first.append((14, 6, at))
        if 1 <= at < CHUNKS:
            first.append((6, 2, at - 1))
            second.append((6, 10, at - 1))
        if 2 <= at <= CHUNKS:
            first += [(2, 0, at - 2), (10, 8, at - 2)]
            second += [(2, 4, at - 2), (10, 12, at - 2)]
        if at == CHUNKS:
            first += [(14, 10, at - 1), (6, 2, at - 1)]
        if at == CHUNKS + 1:
            first += [(14, 12, at - 2), (10, 8, at - 2), (6, 4, at - 2), (2, 0, at - 2)]
        rounds.append((first, second))
    return rounds


def carry_chunks(section_at, transfers, held, own, pairs):
    value = own
    for source, _, c in transfers:
        value = held[c] if value is None else jnp.where(section_at == source, held[c], value)
    pairs = pairs + [
        (device_of(source, r), device_of(target, r))
        for source, target, _ in transfers
        for r in range(ROWS)
    ]
    return lax.ppermute(value, AXES, pairs)


def keep_chunks(section_at, transfers, held, moved):
    for _, target, c in transfers:
        held[c] = jnp.where(section_at == target, moved, held[c])


def activate(tensor):
    return jax.nn.silu(tensor.astype(jnp.float32)).astype(jnp.bfloat16)


def to_everyone(value):
    count = SECTIONS * ROWS
    copies = jnp.broadcast_to(value, (count,) + value.shape[1:])
    return lax.all_to_all(copies, AXES, 0, 0, tiled=True)


def local(
    hidden,
    cond,
    mod_weight,
    mod_bias,
    proj_weight,
    proj_bias,
    latent_cache,
    in_weight,
    in_bias,
    conv_weight,
    conv_bias,
    conv_cache,
    final_weight,
    final_bias,
    final_cache,
):
    section_at = lax.axis_index("section")
    row_at = lax.axis_index("row")
    model_width = hidden.shape[-1]
    own_terms = jnp.dot(activate(cond)[None], mod_weight, preferred_element_type=jnp.float32)[
        0
    ] + mod_bias.astype(jnp.float32)
    own_count = own_terms.shape[0]
    padded_terms = jnp.pad(own_terms, (0, 128 - own_count))[None, None]
    modulation = to_everyone(padded_terms)[:, 0, :own_count].reshape(-1)
    shift_part = modulation[:model_width]
    scale_part = modulation[model_width:]
    values = hidden.astype(jnp.float32)
    average = jnp.mean(values, axis=-1, keepdims=True)
    centered = values - average
    variance = jnp.mean(centered * centered, axis=-1, keepdims=True)
    normed = centered / jnp.sqrt(variance + 1e-06)
    modded = (normed * (1.0 + scale_part) + shift_part).astype(jnp.bfloat16)
    patches = (
        jnp.dot(modded.reshape(-1, model_width), proj_weight, preferred_element_type=jnp.float32)
        + proj_bias.astype(jnp.float32)
    ).astype(jnp.bfloat16)
    lat_chan = latent_cache.shape[-1]
    own_latent = patches.reshape(1, hidden.shape[1], hidden.shape[2], lat_chan, 2, 2)
    own_latent = own_latent.transpose(0, 1, 4, 2, 5, 3).reshape(1, STRIPE, COLS * lat_chan)
    latent_old = latent_cache.reshape(1, 2 * STRIPE, COLS * lat_chan)
    blocks = to_everyone(jnp.concatenate([own_latent, latent_old, own_latent], axis=1))
    at_end = row_at == ROWS - 1

    leans_down = (section_at // 2) % 2 == 0
    offset = jnp.where(leans_down, 0, -2)
    seam = (2 * RING - STRIPE * row_at - offset) % RING
    flags = jnp.stack([section_at, leans_down.astype(jnp.int32), seam, row_at]).astype(jnp.int32)
    own_cache = conv_cache[0].transpose(1, 0, 2, 3).reshape(STRIPE, 2 * COLS, CH)
    last_cache = final_cache.transpose(1, 0, 2, 3).reshape(STRIPE, 2 * COLS, CH)
    above = neighbour_rows(jnp.concatenate([own_cache, last_cache[STRIPE - 1 :]], axis=0), 1)
    below = neighbour_rows(jnp.concatenate([own_cache, last_cache[:1]], axis=0), -1)
    around_cache = jnp.concatenate([above[:STRIPE], own_cache, below[:STRIPE]], axis=0)

    def within(top, bottom):
        return (
            jnp.where(row_at == 0, jnp.zeros_like(top), top),
            jnp.where(at_end, jnp.zeros_like(bottom), bottom),
        )

    top, bottom = within(above[STRIPE:], below[STRIPE:])
    last_history = jnp.concatenate([top, last_cache, bottom], axis=0)
    history_a = lax.dynamic_slice_in_dim(around_cache, STRIPE + offset, WINDOW, axis=0)
    history_b = lax.dynamic_slice_in_dim(around_cache, STRIPE + offset + 1, WIDE, axis=0)
    bias_rows = jnp.broadcast_to(conv_bias[None], (1, 2 * COLS, CH))
    moved = to_even(jnp.concatenate([history_b, bias_rows], axis=0))
    history_b = moved[:WIDE]
    layer_bias = conv_bias.astype(jnp.float32)
    next_bias = moved[WIDE, :1].astype(jnp.float32)

    result, history_a, history_b, entries, layer_weight, next_weight = first_step(
        flags,
        blocks,
        in_weight,
        in_bias.astype(jnp.float32)[None],
        conv_weight[0],
        to_even(conv_weight[0]),
        history_a,
        history_b,
        layer_bias,
        next_bias,
    )
    section_lanes = lax.optimization_barrier(jnp.full((1, 1, CH), section_at, jnp.int32))
    steps = 2 * (STAGES - 1) + CHUNKS
    hops = {}
    held = []
    rounds = spread_plan()
    for step in range(steps):
        entry = entries[step] if step < CHUNKS else None
        main, slant = hops.pop(step, (None, None))
        if step > 0:
            result, history_a, history_b = run_step(
                step,
                flags,
                entry,
                main,
                slant,
                history_a,
                history_b,
                layer_weight,
                next_weight,
                layer_bias,
                next_bias,
            )
        if step < SPREAD_FROM:
            hops[step + 2] = (
                lax.ppermute(result, AXES, straight_pairs(step)),
                lax.ppermute(result, AXES, slanted_pairs(step)),
            )
            continue
        held.append(result)
        first, second = rounds[step - SPREAD_FROM]
        main = carry_chunks(section_lanes, first, held, result, straight_pairs(step))
        if second or slanted_pairs(step):
            slant = carry_chunks(section_lanes, second, held, result, slanted_pairs(step))
            keep_chunks(section_lanes, second, held, slant)
        keep_chunks(section_lanes, first, held, main)
        if straight_pairs(step):
            hops[step + 2] = (main, slant)
    for first, second in rounds[CHUNKS:]:
        moved = carry_chunks(section_lanes, first, held, None, [])
        if second:
            also_moved = carry_chunks(section_lanes, second, held, None, [])
            keep_chunks(section_lanes, second, held, also_moved)
        keep_chunks(section_lanes, first, held, moved)

    second = lax.ppermute(
        history_b, AXES, [(device_of(s, r), device_of(s + 1, r)) for s in EVENS for r in range(ROWS)]
    )
    second_above = lax.ppermute(
        history_b[3:4],
        AXES,
        [
            (device_of(s, r), device_of(s + 1, r + 1))
            for s in EVENS
            if s % 4 == 0
            for r in range(ROWS)
        ],
    )
    first_rows = lax.dynamic_slice_in_dim(history_a, -offset, STRIPE, axis=0)
    second_rows = lax.dynamic_slice_in_dim(
        jnp.concatenate([second_above, second], axis=0), -offset, STRIPE, axis=0
    )
    new_cache = jnp.where(section_at % 2 == 0, first_rows, second_rows)
    new_cache = new_cache.reshape(STRIPE, 2, COLS, CH).transpose(1, 0, 2, 3)[None]

    last_bias = final_bias.astype(jnp.float32)[None]
    value = jnp.concatenate(held, axis=1)
    moved = lax.ppermute(
        value, AXES, [(device_of(s, r), device_of(s + 1, r)) for s in EVENS for r in range(ROWS)]
    )
    value = jnp.where(section_lanes % 2 == 0, value, moved)
    top, bottom = within(neighbour_rows(value[STRIPE - 1 :], 1), neighbour_rows(value[:1], -1))
    decoded, _ = final_part(FRAMES, value, top, bottom, last_history, final_weight.T, last_bias)
    return (decoded, new_cache)


def solution(mesh):
    placed = (
        P("section", "row", None, None),
        P(),
        P(None, ("section", "row")),
        P(("section", "row")),
        P(),
        P(),
        P(None, "row", None, None),
        P(),
        P(),
        P("section", None, None),
        P("section", None),
        P("section", None, "row", None, None),
        P(None, "section"),
        P("section"),
        P(None, "row", None, None),
    )
    return jax.shard_map(
        local,
        mesh=mesh,
        in_specs=placed,
        out_specs=(P(None, "row", None, "section"), P("section", None, "row", None, None)),
        check_vma=False,
    )
```

```python
import functools

import jax
import jax.numpy as jnp
from jax import lax
from jax.experimental import pallas as pl
from jax.experimental.pallas import tpu as pltpu
from jax.sharding import PartitionSpec as P

AXES = ("section", "row")
SECTIONS = 16
ROWS = 8
STRIPE = 4
RING = ROWS * STRIPE
COLS = 8
CH = 512
CHUNK = 4
CHUNKS = 4
LANES = CHUNK * COLS
WINDOW = 8
WIDE = 6
TAP = 3 * CH
VMEM_LIMIT = 24 << 20
ENTRY_VMEM = 14 << 20
STEP_VMEM = 8 << 20
STAGES = SECTIONS // 2
LAST = SECTIONS - 2
SPREAD_FROM = LAST
C_LAT = 16
ROW_LANES = COLS * C_LAT
FRAMES = SECTIONS


def device_of(section, row):
    return section * ROWS + row % ROWS


def sending_stages(step):
    groups = [range(2), range(2, 8), range(8, 12), range(12, SPREAD_FROM)]
    steps = next((group for group in groups if step in group), (step,))
    return [j for j in range(STAGES - 1) if any(0 <= t - 2 * j < CHUNKS for t in steps)]


def section_pairs(way):
    return [(device_of(way[0], r), device_of(way[1], r)) for r in range(ROWS)] if way else []


def straight_pairs(step):
    return [
        (device_of(2 * j, r), device_of(2 * j + 2, r))
        for j in sending_stages(step)
        for r in range(ROWS)
    ]


def slanted_pairs(step):
    return [
        (device_of(2 * j, r), device_of(2 * j + 2, r + (-1 if j % 2 == 0 else 1)))
        for j in sending_stages(step)
        for r in range(ROWS)
    ]


def prepare_rows(count, window, history, history_out, taps):
    lanes = window.shape[1]
    size = lanes + 2 * COLS
    column = lax.broadcasted_iota(jnp.int32, (size, CH), 0) % COLS
    zero = jnp.zeros((size, CH), jnp.float32)

    def prepare(y):
        value = window[y].astype(jnp.float32)
        active = (value / (1.0 + jnp.exp(-value))).astype(jnp.bfloat16)
        frames = jnp.concatenate(
            [history[y].astype(jnp.float32), active.astype(jnp.float32)], axis=0
        )
        history_out[y] = active[lanes - 2 * COLS :]
        before = jnp.where(column == 0, zero, pltpu.roll(frames, 1, 0))
        after = jnp.where(column == COLS - 1, zero, pltpu.roll(frames, size - 1, 0))
        for e, shifted in enumerate((before, frames, after)):
            for a in range(3):
                taps[a * 3 + e, y] = shifted[a * COLS : a * COLS + lanes].astype(jnp.bfloat16)

    def pair(i, carry):
        prepare(2 * i)
        prepare(2 * i + 1)
        return carry

    lax.fori_loop(0, count // 2, pair, 0)


def convolve(rows, seam, taps, saved, total, weight):
    size = rows * LANES

    def add(b):
        def one(a, carry):
            left = jnp.concatenate(
                [taps[a * 3 + e, b : b + rows].reshape(size, CH) for e in range(3)], axis=-1
            )
            at = pl.multiple_of((9 * a + 3 * b) * CH, TAP)
            total[:size] += jnp.dot(
                left, weight[pl.ds(at, TAP), :], preferred_element_type=jnp.float32
            )
            return carry

        lax.fori_loop(0, 3, one, 0)

    add(1)
    at_seam = jnp.logical_and(seam > 0, seam < rows + 2)

    @pl.when(at_seam)
    def _():
        saved[...] = taps[:, seam - 1]
        taps[:, seam - 1] = jnp.zeros((9, LANES, CH), jnp.bfloat16)

    add(0)

    @pl.when(at_seam)
    def _():
        taps[:, seam - 1] = saved[...]
        taps[:, seam] = jnp.zeros((9, LANES, CH), jnp.bfloat16)

    add(2)


def first_block(seam, window, history, new, bias, weight, scratch):
    middle, taps, saved, total = scratch
    prepare_rows(WINDOW, window, history, new, taps)
    inner = window[1 : 1 + WIDE].astype(jnp.float32).reshape(WIDE * LANES, CH)
    total[...] = inner + bias[...]
    convolve(WIDE, seam, taps, saved, total, weight)
    middle[...] = total[...].astype(jnp.bfloat16).reshape(WIDE, LANES, CH)


def second_block(seam, out, history, new, bias, weight, scratch):
    middle, taps, saved, total = scratch
    size = STRIPE * LANES
    prepare_rows(WIDE, middle, history, new, taps)
    inner = middle[1 : 1 + STRIPE].astype(jnp.float32).reshape(size, CH)
    total[:size] = inner + bias[...]
    convolve(STRIPE, seam - 1, taps, saved, total, weight)
    out[...] = total[:size].astype(jnp.bfloat16).reshape(STRIPE, LANES, CH)


STEP_SCRATCH = [
    pltpu.VMEM((WINDOW, LANES, CH), jnp.bfloat16),
    pltpu.VMEM((WIDE, LANES, CH), jnp.bfloat16),
    pltpu.VMEM((9, WINDOW, LANES, CH), jnp.bfloat16),
    pltpu.VMEM((9, LANES, CH), jnp.bfloat16),
    pltpu.VMEM((WIDE * LANES, CH), jnp.float32),
]


def pair_step(step, has_entry, has_hop, flags, *refs):
    refs = list(refs)
    entry = [refs.pop(0) for _ in range(4)] if has_entry else None
    main, slant = (refs.pop(0), refs.pop(0)) if has_hop else (None, None)
    (history_a, history_b, weight_a, weight_b, bias_a, bias_b) = refs[:6]
    (out, new_a, new_b, window, middle, taps, saved, total) = refs[6:14]
    section = flags[0]
    leans_down = flags[1]
    seam = flags[2]
    chunk = step - section

    @pl.when(jnp.logical_and(section % 2 == 0, jnp.logical_and(chunk >= 0, chunk < CHUNKS)))
    def _():
        if has_entry:

            @pl.when(section == 0)
            def _():
                now, past, in_weight, in_bias = entry
                now = (from_tiles if step < 2 else from_packed)(now)
                past = (from_tiles if step < 3 else from_packed)(past)
                make_entry(flags[3], now, past, in_weight, in_bias, window, *refs[14:])

        if has_hop:

            @pl.when(leans_down == 1)
            def _():
                window[:STRIPE] = main[...]
                window[STRIPE:] = slant[...]

            @pl.when(jnp.logical_and(section > 0, leans_down == 0))
            def _():
                window[:STRIPE] = slant[...]
                window[STRIPE:] = main[...]

        scratch = (middle, taps, saved, total)
        first_block(seam, window, history_a, new_a, bias_a, weight_a, scratch)
        second_block(seam, out, history_b, new_b, bias_b, weight_b, scratch)


def run_step(step, flags, entry, main, slant, history_a, history_b, *weights):
    has_entry = entry is not None
    has_hop = main is not None
    arrays = (list(entry) if has_entry else []) + ([main, slant] if has_hop else [])
    at = 1 + len(arrays)
    arrays += [history_a, history_b, *weights]
    vmem = pl.BlockSpec(memory_space=pltpu.VMEM)
    flops = 2 * (WIDE + STRIPE) * LANES * 27 * CH * CH
    return pl.pallas_call(
        functools.partial(pair_step, step, has_entry, has_hop),
        in_specs=[pl.BlockSpec(memory_space=pltpu.SMEM)] + [vmem] * len(arrays),
        out_specs=(vmem,) * 3,
        out_shape=(
            jax.ShapeDtypeStruct((STRIPE, LANES, CH), jnp.bfloat16),
            jax.ShapeDtypeStruct(history_a.shape, jnp.bfloat16),
            jax.ShapeDtypeStruct(history_b.shape, jnp.bfloat16),
        ),
        input_output_aliases={at: 1, at + 1: 2},
        scratch_shapes=STEP_SCRATCH + (ENTRY_SCRATCH if has_entry else []),
        compiler_params=pltpu.CompilerParams(vmem_limit_bytes=STEP_VMEM),
        cost_estimate=pl.CostEstimate(flops=flops, bytes_accessed=1 << 20, transcendentals=0),
        name="pair_step",
    )(flags, *arrays)


def from_tiles(ref):
    return lambda at: ref[at // 4].astype(jnp.float32)[at % 4 * STRIPE : (at % 4 + 1) * STRIPE]


def packed_tile(ref, g):
    first, lane = (0, g * ROW_LANES) if g < 4 else (16, 0)
    return ref.at[0, first : first + 16, lane : lane + ROW_LANES]


def from_packed(ref):
    return lambda at: packed_tile(ref, at // 4)[...].astype(jnp.float32)[
        at % 4 * STRIPE : (at % 4 + 1) * STRIPE
    ]


def make_entry(row, now, past, weight, bias, window, rows, padded, left, total):
    group = CHUNK + 2
    for f in range(group):
        source, at = (past, f + CHUNK) if f < 2 and past is not None else (now, f)
        own, above, below = [source(part * group + at) for part in range(3)]
        pieces = [above[i : i + 1] for i in range(1, STRIPE)]
        pieces += [own[i : i + 1] for i in range(STRIPE)]
        pieces += [below[i : i + 1] for i in range(STRIPE - 1)]
        for i, piece in enumerate(pieces):
            rows[i, f : f + 1] = piece
    padded[...] = jnp.zeros_like(padded)
    for ab in range(9):
        padded[ab * ROW_LANES : ab * ROW_LANES + 3 * C_LAT] = weight[
            ab * 3 * C_LAT : (ab + 1) * 3 * C_LAT
        ]
    frames = 8
    count = WINDOW * frames
    lane = lax.broadcasted_iota(jnp.int32, (2 * frames, ROW_LANES), 1)
    seam = jnp.where(row == 0, 3, jnp.where(row == ROWS - 1, 7, -9))

    def arrange(i, carry):
        for ab in range(9):
            a, b = ab // 3, ab % 3
            both = []
            for y in (2 * i, 2 * i + 1):
                piece = rows[y + b, a : a + frames]
                if b != 1:
                    hidden = y + 1 == (seam if b == 0 else seam - 1)
                    piece = jnp.where(hidden, jnp.zeros_like(piece), piece)
                both.append(piece)
            piece = jnp.concatenate(both, axis=0)
            for x in range(COLS):
                moved = piece if x == 1 else pltpu.roll(piece, (1 - x) * C_LAT % ROW_LANES, 1)
                if x == 0:
                    moved = jnp.where(lane < C_LAT, jnp.zeros_like(moved), moved)
                if x == COLS - 1:
                    moved = jnp.where(lane >= 2 * C_LAT, jnp.zeros_like(moved), moved)
                at = pl.multiple_of(x * count + i * 2 * frames, 2 * frames)
                left[pl.ds(at, 2 * frames), ab * ROW_LANES : (ab + 1) * ROW_LANES] = moved.astype(
                    jnp.bfloat16
                )
        return carry

    lax.fori_loop(0, WINDOW // 2, arrange, 0)
    for x in range(0, COLS, 4):
        value = jnp.dot(
            left[x * count : (x + 4) * count], padded[...], preferred_element_type=jnp.float32
        )
        value = value + bias[...]
        for i in range(4):
            part = value[i * count : (i + 1) * count]
            for q in range(CH // 128):
                total[q, pl.ds(x + i, count, stride=COLS), :] = part[:, q * 128 : q * 128 + 128]
    for y in range(WINDOW):
        at = y * frames * COLS
        for q in range(CH // 128):
            window[y, :, q * 128 : q * 128 + 128] = total[q, at : at + LANES].astype(jnp.bfloat16)


ENTRY_SCRATCH = [
    pltpu.VMEM((STRIPE + 6, 16, ROW_LANES), jnp.float32),
    pltpu.VMEM((9 * ROW_LANES, CH), jnp.bfloat16),
    pltpu.VMEM((COLS * WINDOW * 8, 9 * ROW_LANES), jnp.bfloat16),
    pltpu.VMEM((CH // 128, WINDOW * 8 * COLS, 128), jnp.float32),
]


def first_step_body(
    flags,
    now,
    in_weight,
    in_bias,
    far_a,
    far_b,
    history_a,
    history_b,
    bias_a,
    bias_b,
    out,
    new_a,
    new_b,
    weight_a,
    weight_b,
    rows,
    padded,
    left,
    sums,
    window,
    middle,
    taps,
    saved,
    total,
    done,
):
    section = flags[0]
    seam = flags[2]
    scratch = (middle, taps, saved, total)
    copies = [
        pltpu.make_async_copy(far_a, weight_a, done.at[0]),
        pltpu.make_async_copy(far_b, weight_b, done.at[1]),
    ]
    for copy in copies:
        copy.start()

    @pl.when(section == 0)
    def _():
        make_entry(
            flags[3], from_tiles(now), None, in_weight, in_bias, window, rows, padded, left, sums
        )

    @pl.when(jnp.logical_or(section == 8, section == 12))
    def _():
        for g in range(now.shape[0]):
            packed_tile(out, g)[...] = now[g]

    copies[0].wait()

    @pl.when(section == 0)
    def _():
        first_block(seam, window, history_a, new_a, bias_a, weight_a, scratch)

    copies[1].wait()

    @pl.when(section == 0)
    def _():
        second_block(seam, out, history_b, new_b, bias_b, weight_b, scratch)


def first_step(flags, now, in_weight, in_bias, far_a, far_b, history_a, history_b, *biases):
    vmem = pl.BlockSpec(memory_space=pltpu.VMEM)
    hbm = pl.BlockSpec(memory_space=pltpu.HBM)
    return pl.pallas_call(
        first_step_body,
        in_specs=[pl.BlockSpec(memory_space=pltpu.SMEM)] + [vmem] * 3 + [hbm] * 2 + [vmem] * 4,
        out_specs=(vmem,) * 5,
        out_shape=(
            jax.ShapeDtypeStruct((STRIPE, LANES, CH), jnp.bfloat16),
            jax.ShapeDtypeStruct(history_a.shape, jnp.bfloat16),
            jax.ShapeDtypeStruct(history_b.shape, jnp.bfloat16),
            pltpu.VMEM(far_a.shape, far_a.dtype),
            pltpu.VMEM(far_b.shape, far_b.dtype),
        ),
        input_output_aliases={6: 1, 7: 2},
        scratch_shapes=[
            *ENTRY_SCRATCH,
            *STEP_SCRATCH,
            pltpu.SemaphoreType.DMA((2,)),
        ],
        compiler_params=pltpu.CompilerParams(vmem_limit_bytes=ENTRY_VMEM),
        name="first_step",
    )(
        flags,
        now,
        in_weight,
        in_bias,
        pltpu.with_memory_space_constraint(far_a, pltpu.HBM),
        pltpu.with_memory_space_constraint(far_b, pltpu.HBM),
        history_a,
        history_b,
        *biases,
    )


def final_body(frames, done, flags, rows, history, weight, bias, *refs):
    if done:
        refs[1][:done] = refs[0][...]
        refs = refs[1:]
    (out, new, window, taps, total) = refs
    lanes = frames * COLS
    size = STRIPE * lanes
    window[...] = rows[...]

    @pl.when(flags[3] == 0)
    def _():
        window[0] = jnp.zeros((lanes, CH), jnp.bfloat16)

    @pl.when(flags[3] == ROWS - 1)
    def _():
        window[WIDE - 1] = jnp.zeros((lanes, CH), jnp.bfloat16)

    prepare_rows(WIDE, window, history, new, taps)
    total[...] = jnp.broadcast_to(bias[...], total.shape)

    def one(ab, carry):
        a = ab // 3
        b = ab % 3
        left = jnp.concatenate(
            [taps[a * 3 + e, pl.ds(b, STRIPE)].reshape(size, CH) for e in range(3)], axis=-1
        )
        total[...] += lax.dot_general(
            left,
            weight[:, pl.ds(pl.multiple_of(ab * TAP, TAP), TAP)],
            (((1,), (1,)), ((), ())),
            preferred_element_type=jnp.float32,
        )
        return carry

    lax.fori_loop(0, 9, one, 0)
    for y in range(STRIPE):
        for f in range(frames):
            at = y * lanes + f * COLS
            out[done + f, y] = total[at : at + COLS].astype(jnp.bfloat16)


def final_part(flags, rows, history, weight, bias, *earlier):
    frames = rows.shape[1] // COLS
    done = earlier[0].shape[0] if earlier else 0
    vmem = pl.BlockSpec(memory_space=pltpu.VMEM)
    lanes = frames * COLS
    channels = bias.shape[-1]
    return pl.pallas_call(
        functools.partial(final_body, frames, done),
        in_specs=[pl.BlockSpec(memory_space=pltpu.SMEM)] + [vmem] * (4 + len(earlier)),
        out_specs=(vmem, vmem),
        out_shape=(
            jax.ShapeDtypeStruct((done + frames, STRIPE, COLS, channels), jnp.bfloat16),
            jax.ShapeDtypeStruct(history.shape, jnp.bfloat16),
        ),
        scratch_shapes=[
            pltpu.VMEM((WIDE, lanes, CH), jnp.bfloat16),
            pltpu.VMEM((9, WIDE, lanes, CH), jnp.bfloat16),
            pltpu.VMEM((STRIPE * lanes, channels), jnp.float32),
        ],
        compiler_params=pltpu.CompilerParams(vmem_limit_bytes=VMEM_LIMIT),
        cost_estimate=pl.CostEstimate(
            flops=2 * STRIPE * lanes * 27 * CH * 256, bytes_accessed=1 << 20, transcendentals=0
        ),
        name="final_part",
    )(flags, rows, history, weight, bias, *earlier)


EVENS = range(0, SECTIONS, 2)


def to_even(value):
    return lax.ppermute(
        value, AXES, [(device_of(s + 1, r), device_of(s, r)) for s in EVENS for r in range(ROWS)]
    )


def from_section(value, distance, period):
    pairs = [
        (device_of(s + distance, r), device_of(s, r))
        for s in range(0, SECTIONS, period)
        for r in range(ROWS)
    ]
    return lax.ppermute(value, AXES, pairs)


def neighbour_rows(value, shift):
    return lax.ppermute(
        value,
        AXES,
        [(device_of(s, r), device_of(s, r + shift)) for s in range(SECTIONS) for r in range(ROWS)],
    )


def spread_plan():
    rounds = []
    for at in range(CHUNKS + 2):
        first, second = [], []
        if at < CHUNKS:
            first.append((14, 6, at))
        if 1 <= at < CHUNKS:
            first.append((6, 2, at - 1))
            second.append((6, 10, at - 1))
        if 2 <= at <= CHUNKS:
            first += [(2, 0, at - 2), (10, 8, at - 2)]
            second += [(2, 4, at - 2), (10, 12, at - 2)]
        if at == CHUNKS:
            first += [(14, 10, at - 1), (6, 2, at - 1)]
        if at == CHUNKS + 1:
            first += [(14, 12, at - 2), (10, 8, at - 2), (6, 4, at - 2), (2, 0, at - 2)]
        rounds.append((first, second))
    return rounds


def carry_chunks(section_at, transfers, held, own, pairs):
    value = own
    for source, _, c in transfers:
        value = held[c] if value is None else jnp.where(section_at == source, held[c], value)
    pairs = pairs + [
        (device_of(source, r), device_of(target, r))
        for source, target, _ in transfers
        for r in range(ROWS)
    ]
    return lax.ppermute(value, AXES, pairs)


def keep_chunks(section_at, transfers, held, moved):
    for _, target, c in transfers:
        held[c] = jnp.where(section_at == target, moved, held[c])


def activate(tensor):
    return jax.nn.silu(tensor.astype(jnp.float32)).astype(jnp.bfloat16)


def to_everyone(value):
    count = SECTIONS * ROWS
    copies = jnp.broadcast_to(value, (count,) + value.shape[1:])
    return lax.all_to_all(copies, AXES, 0, 0, tiled=True)


def local(
    hidden,
    cond,
    mod_weight,
    mod_bias,
    proj_weight,
    proj_bias,
    latent_cache,
    in_weight,
    in_bias,
    conv_weight,
    conv_bias,
    conv_cache,
    final_weight,
    final_bias,
    final_cache,
):
    section_at = lax.axis_index("section")
    row_at = lax.axis_index("row")
    model_width = hidden.shape[-1]
    own_terms = jnp.dot(activate(cond)[None], mod_weight, preferred_element_type=jnp.float32)[
        0
    ] + mod_bias.astype(jnp.float32)
    own_count = own_terms.shape[0]
    padded_terms = jnp.pad(own_terms, (0, 128 - own_count))[None, None]
    modulation = to_everyone(padded_terms)[:, 0, :own_count].reshape(-1)
    shift_part = modulation[:model_width]
    scale_part = modulation[model_width:]
    values = hidden.astype(jnp.float32)
    average = jnp.mean(values, axis=-1, keepdims=True)
    centered = values - average
    variance = jnp.mean(centered * centered, axis=-1, keepdims=True)
    normed = centered / jnp.sqrt(variance + 1e-06)
    modded = (normed * (1.0 + scale_part) + shift_part).astype(jnp.bfloat16)
    patches = (
        jnp.dot(modded.reshape(-1, model_width), proj_weight, preferred_element_type=jnp.float32)
        + proj_bias.astype(jnp.float32)
    ).astype(jnp.bfloat16)
    lat_chan = latent_cache.shape[-1]
    own_latent = patches.reshape(1, hidden.shape[1], hidden.shape[2], lat_chan, 2, 2)
    own_latent = own_latent.transpose(0, 1, 4, 2, 5, 3).reshape(1, STRIPE, COLS * lat_chan)
    lane_rows = (-1, STRIPE, COLS * lat_chan)
    two = jnp.concatenate([own_latent, to_even(own_latent)], axis=0)
    four = jnp.concatenate([latent_cache.reshape(lane_rows), two, from_section(two, 2, 4)], axis=0)
    now = [four, neighbour_rows(four, 1), neighbour_rows(four, -1), jnp.zeros_like(four[:2])]
    now = jnp.concatenate(now, axis=0).reshape(-1, 16, COLS * lat_chan)
    one_on = from_section(now, 4, SECTIONS)
    at_end = row_at == ROWS - 1

    leans_down = (section_at // 2) % 2 == 1
    offset = jnp.where(leans_down, 0, -2)
    seam = (2 * RING - STRIPE * row_at - offset) % RING
    flags = jnp.stack([section_at, leans_down.astype(jnp.int32), seam, row_at]).astype(jnp.int32)
    own_cache = conv_cache[0].transpose(1, 0, 2, 3).reshape(STRIPE, 2 * COLS, CH)
    last_cache = final_cache.transpose(1, 0, 2, 3).reshape(STRIPE, 2 * COLS, CH)
    above = neighbour_rows(jnp.concatenate([own_cache, last_cache[STRIPE - 1 :]], axis=0), 1)
    below = neighbour_rows(jnp.concatenate([own_cache, last_cache[:1]], axis=0), -1)
    around_cache = jnp.concatenate([above[:STRIPE], own_cache, below[:STRIPE]], axis=0)

    def within(top, bottom):
        return (
            jnp.where(row_at == 0, jnp.zeros_like(top), top),
            jnp.where(at_end, jnp.zeros_like(bottom), bottom),
        )

    top, bottom = within(above[STRIPE:], below[STRIPE:])
    last_history = jnp.concatenate([top, last_cache, bottom], axis=0)
    history_a = lax.dynamic_slice_in_dim(around_cache, STRIPE + offset, WINDOW, axis=0)
    history_b = lax.dynamic_slice_in_dim(around_cache, STRIPE + offset + 1, WIDE, axis=0)
    bias_rows = jnp.broadcast_to(conv_bias[None], (1, 2 * COLS, CH))
    moved = to_even(jnp.concatenate([history_b, bias_rows], axis=0))
    history_b = moved[:WIDE]
    layer_bias = conv_bias.astype(jnp.float32)
    next_bias = moved[WIDE, :1].astype(jnp.float32)

    entry_bias = in_bias.astype(jnp.float32)[None]
    result, history_a, history_b, layer_weight, next_weight = first_step(
        flags,
        now,
        in_weight,
        entry_bias,
        conv_weight[0],
        to_even(conv_weight[0]),
        history_a,
        history_b,
        layer_bias,
        next_bias,
    )
    section_lanes = lax.optimization_barrier(jnp.full((1, 1, CH), section_at, jnp.int32))
    steps = 2 * (STAGES - 1) + CHUNKS
    hops = {}
    held = []
    rounds = spread_plan()
    for step in range(steps):
        entry = None
        if 0 < step < CHUNKS:
            latents = [now, one_on, *first_hop]
            entry = (latents[step], latents[step - 1], in_weight, entry_bias)
        main, slant = hops.pop(step, (None, None))
        if step > 0:
            result, history_a, history_b = run_step(
                step,
                flags,
                entry,
                main,
                slant,
                history_a,
                history_b,
                layer_weight,
                next_weight,
                layer_bias,
                next_bias,
            )
        if step < SPREAD_FROM:
            also = [(8, 0), (12, 0)] if step == 0 else [None, None]
            hops[step + 2] = (
                lax.ppermute(result, AXES, straight_pairs(step) + section_pairs(also[0])),
                lax.ppermute(result, AXES, slanted_pairs(step) + section_pairs(also[1])),
            )
            if step == 0:
                first_hop = hops[2]
            continue
        held.append(result)
        first, second = rounds[step - SPREAD_FROM]
        main = carry_chunks(section_lanes, first, held, result, straight_pairs(step))
        if second or slanted_pairs(step):
            slant = carry_chunks(section_lanes, second, held, result, slanted_pairs(step))
            keep_chunks(section_lanes, second, held, slant)
        keep_chunks(section_lanes, first, held, main)
        if straight_pairs(step):
            hops[step + 2] = (main, slant)
    early = jnp.concatenate(held[:2], axis=1)
    early = jnp.concatenate([neighbour_rows(early[1:], 1), early[:3]], axis=0)
    for first, second in rounds[CHUNKS:]:
        moved = carry_chunks(section_lanes, first, held, None, [])
        if second:
            also_moved = carry_chunks(section_lanes, second, held, None, [])
            keep_chunks(section_lanes, second, held, also_moved)
        keep_chunks(section_lanes, first, held, moved)
    late = jnp.concatenate(held[2:], axis=1)
    above = neighbour_rows(jnp.concatenate([late[1:], history_b[3:]], axis=1), 1)
    second = jnp.concatenate([above[:1, 2 * LANES :], history_b], axis=0)
    second = lax.dynamic_slice_in_dim(second, -offset, STRIPE, axis=0)
    late = jnp.concatenate([above[:, : 2 * LANES], late[:3]], axis=0)

    def with_odd(rows):
        moved = lax.ppermute(
            rows, AXES, [(device_of(s, r), device_of(s + 1, r)) for s in EVENS for r in range(ROWS)]
        )
        return jnp.where(section_lanes % 2 == 0, rows, moved)

    early = with_odd(early)
    late = with_odd(
        jnp.concatenate([late, jnp.pad(second, ((0, 2), (0, 0), (0, 0)))], axis=1)
    )
    late, second = late[:, : 2 * LANES], late[:STRIPE, 2 * LANES :]

    last_bias = final_bias.astype(jnp.float32)[None]
    closing = (final_weight.T, last_bias)
    decoded, last_history = final_part(flags, early, last_history, *closing)
    decoded, _ = final_part(flags, late, last_history, *closing, decoded)

    first = lax.dynamic_slice_in_dim(history_a, -offset, STRIPE, axis=0)
    new_cache = jnp.where(section_at % 2 == 0, first, second)
    new_cache = new_cache.reshape(STRIPE, 2, COLS, CH).transpose(1, 0, 2, 3)[None]
    return (decoded, new_cache)


def solution(mesh):
    placed = (
        P("section", "row", None, None),
        P(),
        P(None, ("section", "row")),
        P(("section", "row")),
        P(),
        P(),
        P(None, "row", None, None),
        P(),
        P(),
        P("section", None, None),
        P("section", None),
        P("section", None, "row", None, None),
        P(None, "section"),
        P("section"),
        P(None, "row", None, None),
    )
    return jax.shard_map(
        local,
        mesh=mesh,
        in_specs=placed,
        out_specs=(P(None, "row", None, "section"), P("section", None, "row", None, None)),
        check_vma=False,
    )
```

```python
import functools

import jax
import jax.numpy as jnp
from jax import lax
from jax.experimental import pallas as pl
from jax.experimental.pallas import tpu as pltpu
from jax.sharding import PartitionSpec as P

AXES = ("section", "row")
SECTIONS = 16
ROWS = 8
STRIPE = 4
RING = ROWS * STRIPE
COLS = 8
CH = 512
CHUNK = 4
CHUNKS = 4
LANES = CHUNK * COLS
WINDOW = 8
WIDE = 6
TAP = 3 * CH
VMEM_LIMIT = 24 << 20
ENTRY_VMEM = 14 << 20
STEP_VMEM = 8 << 20
STAGES = SECTIONS // 2
LAST = SECTIONS - 2
SPREAD_FROM = LAST
C_LAT = 16
ROW_LANES = COLS * C_LAT
FRAMES = SECTIONS


def device_of(section, row):
    return section * ROWS + row % ROWS


def sending_stages(step):
    groups = [range(2), range(2, 8), range(8, 12), range(12, SPREAD_FROM)]
    steps = next((group for group in groups if step in group), (step,))
    return [j for j in range(STAGES - 1) if any(0 <= t - 2 * j < CHUNKS for t in steps)]


def section_pairs(way):
    return [(device_of(way[0], r), device_of(way[1], r)) for r in range(ROWS)] if way else []


def straight_pairs(step):
    return [
        (device_of(2 * j, r), device_of(2 * j + 2, r))
        for j in sending_stages(step)
        for r in range(ROWS)
    ]


def slanted_pairs(step):
    return [
        (device_of(2 * j, r), device_of(2 * j + 2, r + (-1 if j % 2 == 0 else 1)))
        for j in sending_stages(step)
        for r in range(ROWS)
    ]


def prepare_rows(count, window, history, history_out, taps):
    lanes = window.shape[1]
    size = lanes + 2 * COLS
    column = lax.broadcasted_iota(jnp.int32, (size, CH), 0) % COLS
    zero = jnp.zeros((size, CH), jnp.float32)

    def prepare(y):
        value = window[y].astype(jnp.float32)
        active = (value / (1.0 + jnp.exp(-value))).astype(jnp.bfloat16)
        frames = jnp.concatenate(
            [history[y].astype(jnp.float32), active.astype(jnp.float32)], axis=0
        )
        history_out[y] = active[lanes - 2 * COLS :]
        before = jnp.where(column == 0, zero, pltpu.roll(frames, 1, 0))
        after = jnp.where(column == COLS - 1, zero, pltpu.roll(frames, size - 1, 0))
        for e, shifted in enumerate((before, frames, after)):
            for a in range(3):
                taps[a * 3 + e, y] = shifted[a * COLS : a * COLS + lanes].astype(jnp.bfloat16)

    def pair(i, carry):
        prepare(2 * i)
        prepare(2 * i + 1)
        return carry

    lax.fori_loop(0, count // 2, pair, 0)


def convolve(rows, seam, taps, saved, total, weight):
    size = rows * LANES

    def add(b):
        for a in range(3):
            left = jnp.concatenate(
                [taps[a * 3 + e, b : b + rows].reshape(size, CH) for e in range(3)], axis=-1
            )
            at = (9 * a + 3 * b) * CH
            total[:size] += jnp.dot(
                left, weight[at : at + TAP], preferred_element_type=jnp.float32
            )

    add(1)
    at_seam = jnp.logical_and(seam > 0, seam < rows + 2)

    @pl.when(at_seam)
    def _():
        saved[...] = taps[:, seam - 1]
        taps[:, seam - 1] = jnp.zeros((9, LANES, CH), jnp.bfloat16)

    add(0)

    @pl.when(at_seam)
    def _():
        taps[:, seam - 1] = saved[...]
        taps[:, seam] = jnp.zeros((9, LANES, CH), jnp.bfloat16)

    add(2)


def first_block(seam, window, history, new, bias, weight, scratch):
    middle, taps, saved, total = scratch
    prepare_rows(WINDOW, window, history, new, taps)
    inner = window[1 : 1 + WIDE].astype(jnp.float32).reshape(WIDE * LANES, CH)
    total[...] = inner + bias[...]
    convolve(WIDE, seam, taps, saved, total, weight)
    middle[...] = total[...].astype(jnp.bfloat16).reshape(WIDE, LANES, CH)


def second_block(seam, out, history, new, bias, weight, scratch):
    middle, taps, saved, total = scratch
    size = STRIPE * LANES
    prepare_rows(WIDE, middle, history, new, taps)
    inner = middle[1 : 1 + STRIPE].astype(jnp.float32).reshape(size, CH)
    total[:size] = inner + bias[...]
    convolve(STRIPE, seam - 1, taps, saved, total, weight)
    out[...] = total[:size].astype(jnp.bfloat16).reshape(STRIPE, LANES, CH)


STEP_SCRATCH = [
    pltpu.VMEM((WINDOW, LANES, CH), jnp.bfloat16),
    pltpu.VMEM((WIDE, LANES, CH), jnp.bfloat16),
    pltpu.VMEM((9, WINDOW, LANES, CH), jnp.bfloat16),
    pltpu.VMEM((9, LANES, CH), jnp.bfloat16),
    pltpu.VMEM((WIDE * LANES, CH), jnp.float32),
]


def pair_step(step, has_entry, has_hop, flags, *refs):
    refs = list(refs)
    entry = [refs.pop(0) for _ in range(4)] if has_entry else None
    main, slant = (refs.pop(0), refs.pop(0)) if has_hop else (None, None)
    (history_a, history_b, weight_a, weight_b, bias_a, bias_b) = refs[:6]
    (out, new_a, new_b, window, middle, taps, saved, total) = refs[6:14]
    section = flags[0]
    leans_down = flags[1]
    seam = flags[2]
    chunk = step - section

    @pl.when(jnp.logical_and(section % 2 == 0, jnp.logical_and(chunk >= 0, chunk < CHUNKS)))
    def _():
        if has_entry:

            @pl.when(section == 0)
            def _():
                now, past, in_weight, in_bias = entry
                now = (from_tiles if step < 2 else from_packed)(now)
                past = (from_tiles if step < 3 else from_packed)(past)
                make_entry(flags[3], now, past, in_weight, in_bias, window, *refs[14:])

        if has_hop:

            @pl.when(leans_down == 1)
            def _():
                window[:STRIPE] = main[...]
                window[STRIPE:] = slant[...]

            @pl.when(jnp.logical_and(section > 0, leans_down == 0))
            def _():
                window[:STRIPE] = slant[...]
                window[STRIPE:] = main[...]

        scratch = (middle, taps, saved, total)
        first_block(seam, window, history_a, new_a, bias_a, weight_a, scratch)
        second_block(seam, out, history_b, new_b, bias_b, weight_b, scratch)


def run_step(step, flags, entry, main, slant, history_a, history_b, *weights):
    has_entry = entry is not None
    has_hop = main is not None
    arrays = (list(entry) if has_entry else []) + ([main, slant] if has_hop else [])
    at = 1 + len(arrays)
    arrays += [history_a, history_b, *weights]
    vmem = pl.BlockSpec(memory_space=pltpu.VMEM)
    flops = 2 * (WIDE + STRIPE) * LANES * 27 * CH * CH
    return pl.pallas_call(
        functools.partial(pair_step, step, has_entry, has_hop),
        in_specs=[pl.BlockSpec(memory_space=pltpu.SMEM)] + [vmem] * len(arrays),
        out_specs=(vmem,) * 3,
        out_shape=(
            jax.ShapeDtypeStruct((STRIPE, LANES, CH), jnp.bfloat16),
            jax.ShapeDtypeStruct(history_a.shape, jnp.bfloat16),
            jax.ShapeDtypeStruct(history_b.shape, jnp.bfloat16),
        ),
        input_output_aliases={at: 1, at + 1: 2},
        scratch_shapes=STEP_SCRATCH + (ENTRY_SCRATCH if has_entry else []),
        compiler_params=pltpu.CompilerParams(vmem_limit_bytes=STEP_VMEM),
        cost_estimate=pl.CostEstimate(flops=flops, bytes_accessed=1 << 20, transcendentals=0),
        name="pair_step",
    )(flags, *arrays)


def from_tiles(ref):
    return lambda at: ref[at // 4].astype(jnp.float32)[at % 4 * STRIPE : (at % 4 + 1) * STRIPE]


def packed_tile(ref, g):
    first, lane = (0, g * ROW_LANES) if g < 4 else (16, 0)
    return ref.at[0, first : first + 16, lane : lane + ROW_LANES]


def from_packed(ref):
    return lambda at: packed_tile(ref, at // 4)[...].astype(jnp.float32)[
        at % 4 * STRIPE : (at % 4 + 1) * STRIPE
    ]


def make_entry(row, now, past, weight, bias, window, rows, padded, left, total):
    group = CHUNK + 2
    for f in range(group):
        source, at = (past, f + CHUNK) if f < 2 and past is not None else (now, f)
        own, above, below = [source(part * group + at) for part in range(3)]
        pieces = [above[i : i + 1] for i in range(1, STRIPE)]
        pieces += [own[i : i + 1] for i in range(STRIPE)]
        pieces += [below[i : i + 1] for i in range(STRIPE - 1)]
        for i, piece in enumerate(pieces):
            rows[i, f : f + 1] = piece
    padded[...] = jnp.zeros_like(padded)
    for ab in range(9):
        padded[ab * ROW_LANES : ab * ROW_LANES + 3 * C_LAT] = weight[
            ab * 3 * C_LAT : (ab + 1) * 3 * C_LAT
        ]
    frames = 8
    count = WINDOW * frames
    lane = lax.broadcasted_iota(jnp.int32, (2 * frames, ROW_LANES), 1)
    seam = jnp.where(row == 0, 3, jnp.where(row == ROWS - 1, 7, -9))

    def arrange(i, carry):
        for ab in range(9):
            a, b = ab // 3, ab % 3
            both = []
            for y in (2 * i, 2 * i + 1):
                piece = rows[y + b, a : a + frames]
                if b != 1:
                    hidden = y + 1 == (seam if b == 0 else seam - 1)
                    piece = jnp.where(hidden, jnp.zeros_like(piece), piece)
                both.append(piece)
            piece = jnp.concatenate(both, axis=0)
            for x in range(COLS):
                moved = piece if x == 1 else pltpu.roll(piece, (1 - x) * C_LAT % ROW_LANES, 1)
                if x == 0:
                    moved = jnp.where(lane < C_LAT, jnp.zeros_like(moved), moved)
                if x == COLS - 1:
                    moved = jnp.where(lane >= 2 * C_LAT, jnp.zeros_like(moved), moved)
                at = pl.multiple_of(x * count + i * 2 * frames, 2 * frames)
                left[pl.ds(at, 2 * frames), ab * ROW_LANES : (ab + 1) * ROW_LANES] = moved.astype(
                    jnp.bfloat16
                )
        return carry

    lax.fori_loop(0, WINDOW // 2, arrange, 0)
    for x in range(0, COLS, 4):
        value = jnp.dot(
            left[x * count : (x + 4) * count], padded[...], preferred_element_type=jnp.float32
        )
        value = value + bias[...]
        for i in range(4):
            part = value[i * count : (i + 1) * count]
            for q in range(CH // 128):
                total[q, pl.ds(x + i, count, stride=COLS), :] = part[:, q * 128 : q * 128 + 128]
    for y in range(WINDOW):
        at = y * frames * COLS
        for q in range(CH // 128):
            window[y, :, q * 128 : q * 128 + 128] = total[q, at : at + LANES].astype(jnp.bfloat16)


ENTRY_SCRATCH = [
    pltpu.VMEM((STRIPE + 6, 16, ROW_LANES), jnp.float32),
    pltpu.VMEM((9 * ROW_LANES, CH), jnp.bfloat16),
    pltpu.VMEM((COLS * WINDOW * 8, 9 * ROW_LANES), jnp.bfloat16),
    pltpu.VMEM((CH // 128, WINDOW * 8 * COLS, 128), jnp.float32),
]


def first_step_body(
    flags,
    now,
    in_weight,
    in_bias,
    far_a,
    far_b,
    history_a,
    history_b,
    bias_a,
    bias_b,
    out,
    new_a,
    new_b,
    weight_a,
    weight_b,
    rows,
    padded,
    left,
    sums,
    window,
    middle,
    taps,
    saved,
    total,
    done,
):
    section = flags[0]
    seam = flags[2]
    scratch = (middle, taps, saved, total)
    copies = [
        pltpu.make_async_copy(far_a, weight_a, done.at[0]),
        pltpu.make_async_copy(far_b, weight_b, done.at[1]),
    ]
    for copy in copies:
        copy.start()

    @pl.when(section == 0)
    def _():
        make_entry(
            flags[3], from_tiles(now), None, in_weight, in_bias, window, rows, padded, left, sums
        )

    @pl.when(jnp.logical_or(section == 8, section == 12))
    def _():
        for g in range(now.shape[0]):
            packed_tile(out, g)[...] = now[g]

    copies[0].wait()

    @pl.when(section == 0)
    def _():
        first_block(seam, window, history_a, new_a, bias_a, weight_a, scratch)

    copies[1].wait()

    @pl.when(section == 0)
    def _():
        second_block(seam, out, history_b, new_b, bias_b, weight_b, scratch)


def first_step(flags, now, in_weight, in_bias, far_a, far_b, history_a, history_b, *biases):
    vmem = pl.BlockSpec(memory_space=pltpu.VMEM)
    hbm = pl.BlockSpec(memory_space=pltpu.HBM)
    return pl.pallas_call(
        first_step_body,
        in_specs=[pl.BlockSpec(memory_space=pltpu.SMEM)] + [vmem] * 3 + [hbm] * 2 + [vmem] * 4,
        out_specs=(vmem,) * 5,
        out_shape=(
            jax.ShapeDtypeStruct((STRIPE, LANES, CH), jnp.bfloat16),
            jax.ShapeDtypeStruct(history_a.shape, jnp.bfloat16),
            jax.ShapeDtypeStruct(history_b.shape, jnp.bfloat16),
            pltpu.VMEM(far_a.shape, far_a.dtype),
            pltpu.VMEM(far_b.shape, far_b.dtype),
        ),
        input_output_aliases={6: 1, 7: 2},
        scratch_shapes=[
            *ENTRY_SCRATCH,
            *STEP_SCRATCH,
            pltpu.SemaphoreType.DMA((2,)),
        ],
        compiler_params=pltpu.CompilerParams(vmem_limit_bytes=ENTRY_VMEM),
        name="first_step",
    )(
        flags,
        now,
        in_weight,
        in_bias,
        pltpu.with_memory_space_constraint(far_a, pltpu.HBM),
        pltpu.with_memory_space_constraint(far_b, pltpu.HBM),
        history_a,
        history_b,
        *biases,
    )


def final_body(frames, done, flags, rows, history, weight, bias, *refs):
    if done:
        refs[1][:done] = refs[0][...]
        refs = refs[1:]
    (out, new, window, taps, total) = refs
    lanes = frames * COLS
    size = STRIPE * lanes
    window[...] = rows[...]

    @pl.when(flags[3] == 0)
    def _():
        window[0] = jnp.zeros((lanes, CH), jnp.bfloat16)

    @pl.when(flags[3] == ROWS - 1)
    def _():
        window[WIDE - 1] = jnp.zeros((lanes, CH), jnp.bfloat16)

    prepare_rows(WIDE, window, history, new, taps)
    total[...] = jnp.broadcast_to(bias[...], total.shape)

    for ab in range(9):
        a, b = ab // 3, ab % 3
        left = jnp.concatenate(
            [taps[a * 3 + e, b : b + STRIPE].reshape(size, CH) for e in range(3)], axis=-1
        )
        total[...] += lax.dot_general(
            left,
            weight[:, ab * TAP : (ab + 1) * TAP],
            (((1,), (1,)), ((), ())),
            preferred_element_type=jnp.float32,
        )
    for y in range(STRIPE):
        for f in range(frames):
            at = y * lanes + f * COLS
            out[done + f, y] = total[at : at + COLS].astype(jnp.bfloat16)


def final_part(flags, rows, history, weight, bias, *earlier):
    frames = rows.shape[1] // COLS
    done = earlier[0].shape[0] if earlier else 0
    vmem = pl.BlockSpec(memory_space=pltpu.VMEM)
    lanes = frames * COLS
    channels = bias.shape[-1]
    return pl.pallas_call(
        functools.partial(final_body, frames, done),
        in_specs=[pl.BlockSpec(memory_space=pltpu.SMEM)] + [vmem] * (4 + len(earlier)),
        out_specs=(vmem, vmem),
        out_shape=(
            jax.ShapeDtypeStruct((done + frames, STRIPE, COLS, channels), jnp.bfloat16),
            jax.ShapeDtypeStruct(history.shape, jnp.bfloat16),
        ),
        scratch_shapes=[
            pltpu.VMEM((WIDE, lanes, CH), jnp.bfloat16),
            pltpu.VMEM((9, WIDE, lanes, CH), jnp.bfloat16),
            pltpu.VMEM((STRIPE * lanes, channels), jnp.float32),
        ],
        compiler_params=pltpu.CompilerParams(vmem_limit_bytes=VMEM_LIMIT),
        cost_estimate=pl.CostEstimate(
            flops=2 * STRIPE * lanes * 27 * CH * 256, bytes_accessed=1 << 20, transcendentals=0
        ),
        name="final_part",
    )(flags, rows, history, weight, bias, *earlier)


EVENS = range(0, SECTIONS, 2)


def to_even(value):
    return lax.ppermute(
        value, AXES, [(device_of(s + 1, r), device_of(s, r)) for s in EVENS for r in range(ROWS)]
    )


def from_section(value, distance, period):
    pairs = [
        (device_of(s + distance, r), device_of(s, r))
        for s in range(0, SECTIONS, period)
        for r in range(ROWS)
    ]
    return lax.ppermute(value, AXES, pairs)


def neighbour_rows(value, shift):
    return lax.ppermute(
        value,
        AXES,
        [(device_of(s, r), device_of(s, r + shift)) for s in range(SECTIONS) for r in range(ROWS)],
    )


def spread_plan():
    rounds = []
    for at in range(CHUNKS + 2):
        first, second = [], []
        if at < CHUNKS:
            first.append((14, 6, at))
        if 1 <= at < CHUNKS:
            first.append((6, 2, at - 1))
            second.append((6, 10, at - 1))
        if 2 <= at <= CHUNKS:
            first += [(2, 0, at - 2), (10, 8, at - 2)]
            second += [(2, 4, at - 2), (10, 12, at - 2)]
        if at == CHUNKS:
            first += [(14, 10, at - 1), (6, 2, at - 1)]
        if at == CHUNKS + 1:
            first += [(14, 12, at - 2), (10, 8, at - 2), (6, 4, at - 2), (2, 0, at - 2)]
        rounds.append((first, second))
    return rounds


def carry_chunks(section_at, transfers, held, own, pairs):
    value = own
    for source, _, c in transfers:
        value = held[c] if value is None else jnp.where(section_at == source, held[c], value)
    pairs = pairs + [
        (device_of(source, r), device_of(target, r))
        for source, target, _ in transfers
        for r in range(ROWS)
    ]
    return lax.ppermute(value, AXES, pairs)


def keep_chunks(section_at, transfers, held, moved):
    for _, target, c in transfers:
        held[c] = jnp.where(section_at == target, moved, held[c])


def activate(tensor):
    return jax.nn.silu(tensor.astype(jnp.float32)).astype(jnp.bfloat16)


def to_everyone(value):
    count = SECTIONS * ROWS
    copies = jnp.broadcast_to(value, (count,) + value.shape[1:])
    return lax.all_to_all(copies, AXES, 0, 0, tiled=True)


def local(
    hidden,
    cond,
    mod_weight,
    mod_bias,
    proj_weight,
    proj_bias,
    latent_cache,
    in_weight,
    in_bias,
    conv_weight,
    conv_bias,
    conv_cache,
    final_weight,
    final_bias,
    final_cache,
):
    section_at = lax.axis_index("section")
    row_at = lax.axis_index("row")
    model_width = hidden.shape[-1]
    own_terms = jnp.dot(activate(cond)[None], mod_weight, preferred_element_type=jnp.float32)[
        0
    ] + mod_bias.astype(jnp.float32)
    own_count = own_terms.shape[0]
    padded_terms = jnp.pad(own_terms, (0, 128 - own_count))[None, None]
    modulation = to_everyone(padded_terms)[:, 0, :own_count].reshape(-1)
    shift_part = modulation[:model_width]
    scale_part = modulation[model_width:]
    values = hidden.astype(jnp.float32)
    average = jnp.mean(values, axis=-1, keepdims=True)
    centered = values - average
    variance = jnp.mean(centered * centered, axis=-1, keepdims=True)
    normed = centered / jnp.sqrt(variance + 1e-06)
    modded = (normed * (1.0 + scale_part) + shift_part).astype(jnp.bfloat16)
    patches = (
        jnp.dot(modded.reshape(-1, model_width), proj_weight, preferred_element_type=jnp.float32)
        + proj_bias.astype(jnp.float32)
    ).astype(jnp.bfloat16)
    lat_chan = latent_cache.shape[-1]
    own_latent = patches.reshape(1, hidden.shape[1], hidden.shape[2], lat_chan, 2, 2)
    own_latent = own_latent.transpose(0, 1, 4, 2, 5, 3).reshape(1, STRIPE, COLS * lat_chan)
    lane_rows = (-1, STRIPE, COLS * lat_chan)
    two = jnp.concatenate([own_latent, to_even(own_latent)], axis=0)
    four = jnp.concatenate([latent_cache.reshape(lane_rows), two, from_section(two, 2, 4)], axis=0)
    now = [four, neighbour_rows(four, 1), neighbour_rows(four, -1), jnp.zeros_like(four[:2])]
    now = jnp.concatenate(now, axis=0).reshape(-1, 16, COLS * lat_chan)
    one_on = from_section(now, 4, SECTIONS)
    at_end = row_at == ROWS - 1

    leans_down = (section_at // 2) % 2 == 1
    offset = jnp.where(leans_down, 0, -2)
    seam = (2 * RING - STRIPE * row_at - offset) % RING
    flags = jnp.stack([section_at, leans_down.astype(jnp.int32), seam, row_at]).astype(jnp.int32)
    own_cache = conv_cache[0].transpose(1, 0, 2, 3).reshape(STRIPE, 2 * COLS, CH)
    last_cache = final_cache.transpose(1, 0, 2, 3).reshape(STRIPE, 2 * COLS, CH)
    above = neighbour_rows(jnp.concatenate([own_cache, last_cache[STRIPE - 1 :]], axis=0), 1)
    below = neighbour_rows(jnp.concatenate([own_cache, last_cache[:1]], axis=0), -1)
    around_cache = jnp.concatenate([above[:STRIPE], own_cache, below[:STRIPE]], axis=0)

    def within(top, bottom):
        return (
            jnp.where(row_at == 0, jnp.zeros_like(top), top),
            jnp.where(at_end, jnp.zeros_like(bottom), bottom),
        )

    top, bottom = within(above[STRIPE:], below[STRIPE:])
    last_history = jnp.concatenate([top, last_cache, bottom], axis=0)
    history_a = lax.dynamic_slice_in_dim(around_cache, STRIPE + offset, WINDOW, axis=0)
    history_b = lax.dynamic_slice_in_dim(around_cache, STRIPE + offset + 1, WIDE, axis=0)
    bias_rows = jnp.broadcast_to(conv_bias[None], (1, 2 * COLS, CH))
    moved = to_even(jnp.concatenate([history_b, bias_rows], axis=0))
    history_b = moved[:WIDE]
    layer_bias = conv_bias.astype(jnp.float32)
    next_bias = moved[WIDE, :1].astype(jnp.float32)

    entry_bias = in_bias.astype(jnp.float32)[None]
    result, history_a, history_b, layer_weight, next_weight = first_step(
        flags,
        now,
        in_weight,
        entry_bias,
        conv_weight[0],
        to_even(conv_weight[0]),
        history_a,
        history_b,
        layer_bias,
        next_bias,
    )
    section_lanes = lax.optimization_barrier(jnp.full((1, 1, CH), section_at, jnp.int32))
    steps = 2 * (STAGES - 1) + CHUNKS
    hops = {}
    held = []
    rounds = spread_plan()
    for step in range(steps):
        entry = None
        if 0 < step < CHUNKS:
            latents = [now, one_on, *first_hop]
            entry = (latents[step], latents[step - 1], in_weight, entry_bias)
        main, slant = hops.pop(step, (None, None))
        if step > 0:
            result, history_a, history_b = run_step(
                step,
                flags,
                entry,
                main,
                slant,
                history_a,
                history_b,
                layer_weight,
                next_weight,
                layer_bias,
                next_bias,
            )
        if step < SPREAD_FROM:
            also = [(8, 0), (12, 0)] if step == 0 else [None, None]
            hops[step + 2] = (
                lax.ppermute(result, AXES, straight_pairs(step) + section_pairs(also[0])),
                lax.ppermute(result, AXES, slanted_pairs(step) + section_pairs(also[1])),
            )
            if step == 0:
                first_hop = hops[2]
            continue
        held.append(result)
        first, second = rounds[step - SPREAD_FROM]
        main = carry_chunks(section_lanes, first, held, result, straight_pairs(step))
        if second or slanted_pairs(step):
            slant = carry_chunks(section_lanes, second, held, result, slanted_pairs(step))
            keep_chunks(section_lanes, second, held, slant)
        keep_chunks(section_lanes, first, held, main)
        if straight_pairs(step):
            hops[step + 2] = (main, slant)
    early = jnp.concatenate(held[:2], axis=1)
    early = jnp.concatenate([neighbour_rows(early[1:], 1), early[:3]], axis=0)
    for first, second in rounds[CHUNKS:]:
        moved = carry_chunks(section_lanes, first, held, None, [])
        if second:
            also_moved = carry_chunks(section_lanes, second, held, None, [])
            keep_chunks(section_lanes, second, held, also_moved)
        keep_chunks(section_lanes, first, held, moved)
    late = jnp.concatenate(held[2:], axis=1)
    above = neighbour_rows(jnp.concatenate([late[1:], history_b[3:]], axis=1), 1)
    second = jnp.concatenate([above[:1, 2 * LANES :], history_b], axis=0)
    second = lax.dynamic_slice_in_dim(second, -offset, STRIPE, axis=0)
    late = jnp.concatenate([above[:, : 2 * LANES], late[:3]], axis=0)

    def with_odd(rows):
        moved = lax.ppermute(
            rows, AXES, [(device_of(s, r), device_of(s + 1, r)) for s in EVENS for r in range(ROWS)]
        )
        return jnp.where(section_lanes % 2 == 0, rows, moved)

    early = with_odd(early)
    late = with_odd(
        jnp.concatenate([late, jnp.pad(second, ((0, 2), (0, 0), (0, 0)))], axis=1)
    )
    late, second = late[:, : 2 * LANES], late[:STRIPE, 2 * LANES :]

    last_bias = final_bias.astype(jnp.float32)[None]
    closing = (final_weight.T, last_bias)
    decoded, last_history = final_part(flags, early, last_history, *closing)
    decoded, _ = final_part(flags, late, last_history, *closing, decoded)

    first = lax.dynamic_slice_in_dim(history_a, -offset, STRIPE, axis=0)
    new_cache = jnp.where(section_at % 2 == 0, first, second)
    new_cache = new_cache.reshape(STRIPE, 2, COLS, CH).transpose(1, 0, 2, 3)[None]
    return (decoded, new_cache)


def solution(mesh):
    placed = (
        P("section", "row", None, None),
        P(),
        P(None, ("section", "row")),
        P(("section", "row")),
        P(),
        P(),
        P(None, "row", None, None),
        P(),
        P(),
        P("section", None, None),
        P("section", None),
        P("section", None, "row", None, None),
        P(None, "section"),
        P("section"),
        P(None, "row", None, None),
    )
    return jax.shard_map(
        local,
        mesh=mesh,
        in_specs=placed,
        out_specs=(P(None, "row", None, "section"), P("section", None, "row", None, None)),
        check_vma=False,
    )
```
